128 devices in a mesh: group: 8 (over y, core), tp: 16 (over z, x).
Axes of the slice: x: 4, y: 4, z: 4, core: 2. Of those that a mesh axis runs over, the one named last changes fastest.
Arguments:
- vision_rows: bfloat16 [8, 16, 32, 7680], P('group', None, None, 'tp'), may hold values from -6 to 6
- tile_count: int32 [32], replicated, may hold values from 1 to 4, as said below
- tile_source: int32 [8, 16], replicated, may hold values from 0 to 15, as said below
- row_request: int32 [8, 64], P('group'), may hold values from 0 to 3
- proj_weight: bfloat16 [7680, 8192], P(None, 'tp'), may hold values from -0.0625 to 0.0625
- proj_bias: bfloat16 [8192], P('tp'), may hold values from -3 to 3
- kv_weight: bfloat16 [2, 8192, 1024], P(None, 'tp'), may hold values from -0.0625 to 0.0625
- query_weight: bfloat16 [8192, 8192], P(None, 'tp'), may hold values from -4 to 4
- out_weight: bfloat16 [8192, 8192], P('tp'), may hold values from -0.0625 to 0.0625
- norm_gain: bfloat16 [8192], P('tp'), may hold values from 0.25 to 1.75
- attn_gate: float32 [], replicated, may hold values from 0.5 to 1.5
- states: bfloat16 [2, 512, 8192], P(None, 'group', 'tp'), may hold values from -6 to 6
Outputs:
- mixed: bfloat16 [2, 512, 8192], P(None, 'group', 'tp')
The draws below stay inside these ranges and needn't reach their ends.
Inputs may be any that keep to these rules, and one draw needn't show every extreme that they name: `tile_count`: some request has 4 tiles and some has 1. `tile_source`: each row is a permutation of 0 to 15.
All inputs are finite; a program needn't handle non-finite values.
Results may differ from the reference program's by a relative error of at most 0.02.
Values may be sent and summed in bfloat16 or wider, within the bound.
No kernel may reach another device: no remote copies, remote signals or barrier semaphores. Data moves between devices by JAX's collectives and lax.ppermute only.
A program may use at most 128 MiB of HBM per device.

```python
import math
import jax
import jax.numpy as jnp
from jax import lax

D = 8192
HEADS = 64
KV_HEADS = 8
HEAD_DIM = 128
VD = 7680
MAXT = 4
TILES_DEV = 2
TILE_ROWS = 32
BATCH = 64
STEPS = 2
SLOTS = 16
REQ_GRP = 4
REQS = 32
GROUP_ROWS = 512
N_GROUP = 8


def draw_tile_count(key, part):
    key = jax.random.fold_in(key, 11)
    first, second = jax.random.split(key, 2)
    counts = jax.random.randint(first, (REQS,), 1, MAXT + 1)
    where_full = jax.random.randint(second, (), 0, REQS)
    counts = counts.at[where_full].set(MAXT)
    counts = counts.at[(where_full + 1) % REQS].set(1)
    return counts.astype(jnp.int32)


def draw_tile_source(key, part):
    key = jax.random.fold_in(key, 23)
    keys = jax.random.split(key, N_GROUP)
    orders = jax.vmap(lambda single: jax.random.permutation(single, SLOTS))(keys)
    return orders.astype(jnp.int32)


def draw_query_weight(key, part):
    key = jax.random.fold_in(key, 37)
    first, second, third, fourth = jax.random.split(key, 4)
    chosen = jax.random.randint(second, (HEADS,), 0, 10) < 3
    forced = jnp.arange(HEADS) == jax.random.randint(fourth, (), 0, HEADS)
    chosen = chosen | forced
    base = jax.random.truncated_normal(first, -4.5, 4.5, (D, D), jnp.float32)
    strength = jnp.exp(jax.random.uniform(third, (HEADS,), jnp.float32, math.log(25.0), math.log(80.0)))
    head_scale = jnp.where(chosen, strength, 1.0)
    column_scale = jnp.repeat(head_scale, HEAD_DIM)
    values = base * D ** (-0.5) * column_scale[None, :]
    return jnp.clip(values, -4.0, 4.0).astype(jnp.bfloat16)


def set_ends(values, rng, smallest, high):
    longest = values.shape.index(max(values.shape))
    spots = []
    for shift in (0, 1):
        where = [jax.random.randint(jax.random.fold_in(rng, axis), (), 0, length) for axis, length in enumerate(values.shape)]
        where[longest] = (where[longest] + shift) % values.shape[longest]
        spots.append(tuple(where))
    return values.at[spots[0]].set(smallest).at[spots[1]].set(high)


def block_scale(key, shape, shards, low, high):
    def one(dim, blocks):
        draws = jax.random.uniform(jax.random.fold_in(jax.random.fold_in(key, 6), dim), (blocks,), jnp.float32, low / len(shards), high / len(shards))
        return jnp.repeat(jnp.exp(draws), shape[dim] // blocks).reshape((-1,) + (1,) * (len(shape) - dim - 1))

    factor_of = one(*shards[0])
    for cut in shards[1:]:
        factor_of = factor_of * one(*cut)
    return factor_of


def bell_draw(own_key, extent, deviation, most, shards=(), kind=jnp.bfloat16):
    result = deviation * jax.random.normal(own_key, extent, jnp.float32)
    if shards:
        result = result * block_scale(own_key, extent, shards, -0.22, 0.18)
    return jnp.clip(result, -most, most).astype(kind)


def setup_inputs(seed: int = 0) -> dict:
    arg_keys = jax.random.split(jax.random.key(seed), 13)
    return {
        "vision_rows": bell_draw(arg_keys[0], (N_GROUP, N_GROUP * TILES_DEV, TILE_ROWS, VD), 1.0, 6.0, ((0, 8), (3, 16))),
        "tile_count": draw_tile_count(jax.random.fold_in(arg_keys[12], 71), 0),
        "tile_source": draw_tile_source(jax.random.fold_in(arg_keys[12], 71), 0),
        "row_request": set_ends(jax.random.randint(arg_keys[3], (N_GROUP, BATCH), 0, REQ_GRP), jax.random.fold_in(arg_keys[3], 1), 0, REQ_GRP - 1).astype(jnp.int32),
        "proj_weight": bell_draw(arg_keys[4], (VD, D), VD ** -0.5, 0.0625, ((1, 16),)),
        "proj_bias": bell_draw(arg_keys[5], (D,), 0.5, 3.0, ((0, 16),)),
        "kv_weight": bell_draw(arg_keys[6], (2, D, KV_HEADS * HEAD_DIM), D ** -0.5, 0.0625, ((1, 16),)),
        "query_weight": draw_query_weight(jax.random.fold_in(arg_keys[12], 71), 0),
        "out_weight": bell_draw(arg_keys[8], (D, D), D ** -0.5, 0.0625, ((0, 16),)),
        "norm_gain": jnp.clip(1.0 + 0.15 * jax.random.normal(arg_keys[9], (D,), jnp.float32), 0.25, 1.75).astype(jnp.bfloat16),
        "attn_gate": jnp.clip(jax.random.uniform(arg_keys[10], (), jnp.float32, 0.5, 1.5), 0.5, 1.5),
        "states": bell_draw(arg_keys[11], (STEPS, N_GROUP * BATCH, D), 1.0, 6.0, ((1, 8), (2, 16))),
    }


def reference(vision_rows, tile_count, tile_source, row_request, proj_weight, proj_bias, kv_weight, query_weight, out_weight, norm_gain, attn_gate, states):
    group_size = HEADS // KV_HEADS
    scale = 1.0 / HEAD_DIM ** 0.5
    gate = jnp.tanh(attn_gate.astype(jnp.float32))
    position = jnp.arange(GROUP_ROWS) // TILE_ROWS
    request = position // MAXT
    results = []
    for step in range(STEPS):
        pieces = []
        for group in range(N_GROUP):
            pieces.append(None)
        results.append(pieces)
    for group in range(N_GROUP):
        tiles = vision_rows[:, group * TILES_DEV:(group + 1) * TILES_DEV].reshape(SLOTS, TILE_ROWS, VD)
        rows = tiles[tile_source[group]].reshape(GROUP_ROWS, VD)
        projected = (jnp.dot(rows, proj_weight, preferred_element_type=jnp.float32) + proj_bias.astype(jnp.float32)).astype(jnp.bfloat16)
        keys = jnp.dot(projected, kv_weight[0], preferred_element_type=jnp.float32).astype(jnp.bfloat16).reshape(GROUP_ROWS, KV_HEADS, HEAD_DIM)
        values = jnp.dot(projected, kv_weight[1], preferred_element_type=jnp.float32).astype(jnp.bfloat16).reshape(GROUP_ROWS, KV_HEADS, HEAD_DIM)
        counts = tile_count[group * REQ_GRP + request]
        valid = position % MAXT < counts
        allowed = valid[None, :] & (request[None, :] == row_request[group][:, None])
        for step in range(STEPS):
            hidden = states[step, group * BATCH:(group + 1) * BATCH].astype(jnp.float32)
            square = lax.optimization_barrier(jnp.mean(hidden * hidden, axis=1, keepdims=True))
            normed = (hidden * lax.rsqrt(square + 1e-05) * norm_gain.astype(jnp.float32)).astype(jnp.bfloat16)
            queries = jnp.dot(normed, query_weight, preferred_element_type=jnp.float32).astype(jnp.bfloat16)
            queries = queries.reshape(BATCH, KV_HEADS, group_size, HEAD_DIM)
            scores = jnp.einsum('bkgd,rkd->bkgr', queries.astype(jnp.float32), keys.astype(jnp.float32)) * scale
            masked = allowed[:, None, None, :]
            largest = lax.optimization_barrier(jnp.max(jnp.where(masked, scores, -1e+30), axis=-1, keepdims=True))
            weights = jnp.where(masked, jnp.exp(scores - largest), 0.0)
            total = lax.optimization_barrier(jnp.sum(weights, axis=-1))
            rounded = weights.astype(jnp.bfloat16).astype(jnp.float32)
            summed = jnp.einsum('bkgr,rkd->bkgd', rounded, values.astype(jnp.float32))
            context = (summed / total[..., None]).astype(jnp.bfloat16).reshape(BATCH, D)
            branch = jnp.dot(context, out_weight, preferred_element_type=jnp.float32)
            results[step][group] = (hidden + gate * branch).astype(jnp.bfloat16)
    return jnp.stack([jnp.concatenate(results[step], axis=0) for step in range(STEPS)], axis=0)
```

```python
import functools

import jax
import jax.numpy as jnp
from jax import lax
from jax.experimental import pallas as pl
from jax.experimental.pallas import tpu as pltpu
from jax.sharding import Mesh, PartitionSpec as P

D = 8192
HEADS = 64
KV_HEADS = 8
HEAD_DIM = 128
MAXT = 4
STEPS = 2
F32 = jnp.float32
BF16 = jnp.bfloat16
TP = ("z", "xh", "pr")


def kv_kernel(rows_ref, key_ref, value_ref, out_ref):
    half = out_ref.shape[1]
    weight = jnp.concatenate([key_ref[0], value_ref[0]], axis=1)
    part = jnp.dot(rows_ref[...], weight, preferred_element_type=F32).astype(BF16)
    out_ref[0] = part[:half]
    out_ref[1] = part[half:]


def kv_partials(projected, kv_weight):
    rows, width = projected.shape
    return pl.pallas_call(
        kv_kernel,
        grid=(KV_HEADS,),
        in_specs=[
            pl.BlockSpec((rows, width), lambda h: (0, 0)),
            pl.BlockSpec((1, width, HEAD_DIM), lambda h: (0, 0, h)),
            pl.BlockSpec((1, width, HEAD_DIM), lambda h: (1, 0, h)),
        ],
        out_specs=pl.BlockSpec((2, rows // 2, 2 * HEAD_DIM), lambda h: (h, 0, 0)),
        out_shape=jax.ShapeDtypeStruct((2 * KV_HEADS, rows // 2, 2 * HEAD_DIM), BF16),
        compiler_params=pltpu.CompilerParams(vmem_limit_bytes=32 * 1024 * 1024),
        cost_estimate=pl.CostEstimate(
            flops=2 * rows * width * KV_HEADS * 2 * HEAD_DIM,
            bytes_accessed=8 * 1024 * 1024,
            transcendentals=0,
        ),
    )(projected, kv_weight, kv_weight)


def attend_kernel(query_ref, kv_ref, row_ref, col_ref, weight_ref, out_ref, context_ref):
    batch, width = context_ref.shape

    @pl.when(pl.program_id(0) == 0)
    def _():
        keys = kv_ref[:, :HEAD_DIM]
        values = kv_ref[:, HEAD_DIM:]
        allowed = row_ref[...] == col_ref[...]
        for head in range(width // HEAD_DIM):
            span = slice(head * HEAD_DIM, (head + 1) * HEAD_DIM)
            scores = lax.dot_general(
                query_ref[:, span], keys, (((1,), (1,)), ((), ())), preferred_element_type=F32
            ) * (1.0 / HEAD_DIM**0.5)
            scores = jnp.where(allowed, scores, -1e30)
            largest = jnp.max(scores, axis=1, keepdims=True)
            weights = jnp.where(allowed, jnp.exp(scores - largest), 0.0)
            total = jnp.sum(weights, axis=1, keepdims=True)
            summed = jnp.dot(weights.astype(BF16), values, preferred_element_type=F32)
            context_ref[:, span] = (summed / total).astype(BF16)

    out_ref[0] = jnp.dot(
        context_ref[...], weight_ref[...], preferred_element_type=F32
    ).astype(BF16)


def attend(query, kv, row_request, col_request, out_weight, ranks):
    batch, width = query.shape
    rows = kv.shape[0]
    columns = out_weight.shape[1] // ranks
    return pl.pallas_call(
        attend_kernel,
        grid=(ranks,),
        in_specs=[
            pl.BlockSpec((batch, width), lambda j: (0, 0)),
            pl.BlockSpec((rows, 2 * HEAD_DIM), lambda j: (0, 0)),
            pl.BlockSpec((batch, 1), lambda j: (0, 0)),
            pl.BlockSpec((1, rows), lambda j: (0, 0)),
            pl.BlockSpec((width, columns), lambda j: (0, j)),
        ],
        out_specs=pl.BlockSpec((1, batch, columns), lambda j: (j, 0, 0)),
        out_shape=jax.ShapeDtypeStruct((ranks, batch, columns), BF16),
        scratch_shapes=[pltpu.VMEM((batch, width), BF16)],
        compiler_params=pltpu.CompilerParams(vmem_limit_bytes=32 * 1024 * 1024),
        cost_estimate=pl.CostEstimate(
            flops=2 * batch * width * out_weight.shape[1],
            bytes_accessed=12 * 1024 * 1024,
            transcendentals=batch * rows * 4,
        ),
    )(query, kv, row_request, col_request, out_weight)


def body(
    vision_rows,
    tile_count,
    tile_source,
    row_request,
    proj_weight,
    proj_bias,
    kv_weight,
    query_weight,
    out_weight,
    norm_gain,
    attn_gate,
    states,
):
    groups = lax.axis_size("group")
    ranks = lax.axis_size(TP)
    group = lax.axis_index("group")
    tile_rows, features = vision_rows.shape[2:]
    per_group = vision_rows.shape[1] // groups
    slots = groups * per_group
    group_rows = slots * tile_rows
    req_grp = slots // MAXT
    batch = states.shape[1]
    width = states.shape[2]

    with jax.named_scope("gather_rows"):
        mine = vision_rows[0].reshape(groups, per_group, tile_rows, features)
        mine = mine.transpose(1, 0, 2, 3).reshape(group_rows, features)
        every = lax.all_gather(mine, TP, axis=1, tiled=True)

    with jax.named_scope("query"):
        local = states.reshape(STEPS * batch, width)
        gain_rows = jnp.broadcast_to(norm_gain[None, :], (16, width))
        sent = jnp.concatenate([local, gain_rows], axis=0)
        sent = jnp.broadcast_to(sent[None], (ranks,) + sent.shape)
        full = lax.all_to_all(sent, TP, 0, 0)
        hidden = full[:, : STEPS * batch].astype(F32)
        gain = full[:, STEPS * batch].astype(F32)
        squares = jnp.sum(hidden * hidden, axis=(0, 2))
        inverse = lax.rsqrt(squares / D + 1e-05)
        normed = (hidden * inverse[None, :, None] * gain[:, None, :]).astype(BF16)
        normed = normed.transpose(1, 0, 2).reshape(STEPS * batch, D)
        query = jnp.dot(normed, query_weight, preferred_element_type=F32).astype(BF16)

    with jax.named_scope("project"):
        accum = jnp.dot(every, proj_weight, preferred_element_type=F32)
        projected = (accum + proj_bias.astype(F32)).astype(BF16)

    with jax.named_scope("kv"):
        partial = kv_partials(projected, kv_weight)
        partial = lax.all_to_all(partial, TP, 0, 0)
        kv = jnp.sum(partial.astype(F32), axis=0).astype(BF16)
        kv = kv.reshape(groups, 1, tile_rows, 2 * HEAD_DIM)
        kv = jnp.broadcast_to(kv, (groups, 2, tile_rows, 2 * HEAD_DIM))
        kv = kv.reshape(slots, tile_rows, 2 * HEAD_DIM)
        kv = lax.all_to_all(kv, ("group", "pr"), 0, 0)
        kv = kv.reshape(group_rows, 2 * HEAD_DIM)

    with jax.named_scope("mask"):
        sources = lax.dynamic_index_in_dim(tile_source, group, 0, keepdims=False)
        counts = lax.dynamic_slice_in_dim(tile_count, group * req_grp, req_grp, 0)
        places = jnp.arange(slots, dtype=jnp.int32)
        request = places // MAXT
        valid = places % MAXT < jnp.repeat(counts, MAXT)
        label = jnp.where(valid, request, -1)
        hits = sources[None, :] == places[:, None]
        tile_label = jnp.sum(jnp.where(hits, label[None, :], 0), axis=1)
        col_request = jnp.repeat(tile_label, tile_rows)[None, :]
        rows = jnp.concatenate([row_request[0]] * STEPS)[:, None]

    with jax.named_scope("attend"):
        branch = attend(query, kv, rows, col_request, out_weight, ranks)

    with jax.named_scope("mix"):
        branch = lax.all_to_all(branch, TP, 0, 0)
        reduced = jnp.sum(branch.astype(F32), axis=0)
        mixed = local.astype(F32) + jnp.tanh(attn_gate) * reduced
        return mixed.astype(BF16).reshape(STEPS, batch, width)


def solution(mesh):
    groups = mesh.shape["group"]
    split = Mesh(mesh.devices.reshape(groups, 4, 2, 2), ("group",) + TP)
    in_specs = (
        P("group", None, None, TP),
        P(),
        P(),
        P("group", None),
        P(None, TP),
        P(TP),
        P(None, TP, None),
        P(None, TP),
        P(TP, None),
        P(TP),
        P(),
        P(None, "group", TP),
    )
    out_specs = P(None, "group", TP)
    return jax.shard_map(body, mesh=split, in_specs=in_specs, out_specs=out_specs, check_vma=False)
```

```python
import functools

import jax
import jax.numpy as jnp
from jax import lax
from jax.experimental import pallas as pl
from jax.experimental.pallas import tpu as pltpu
from jax.sharding import Mesh, PartitionSpec as P

D = 8192
HEADS = 64
KV_HEADS = 8
HEAD_DIM = 128
MAXT = 4
STEPS = 2
SIDE = 4
F32 = jnp.float32
BF16 = jnp.bfloat16
TP = ("z", "xh", "pr")
X = ("xh", "pr")
Z = "z"
VMEM = 40 * 1024 * 1024


def shift(value, axis, by):
    return lax.ppermute(value, axis, [(i, (i + by) % SIDE) for i in range(SIDE)])


def project_kernel(spans, final, index_ref, *refs):
    blocks = refs[: len(spans)]
    weight_ref, start_ref, out_ref, accum_ref = refs[len(spans) :]
    step = pl.program_id(0)

    @pl.when(step == 0)
    def _():
        accum_ref[...] = jnp.broadcast_to(start_ref[...], accum_ref.shape)

    for block, (begin, count, half) in zip(blocks, spans):

        @pl.when((step >= begin) & (step < begin + count))
        def _():
            accum_ref[half] += jnp.dot(block[0], weight_ref[0], preferred_element_type=F32)

    @pl.when(step == pl.num_programs(0) - 1)
    def _():
        out_ref[...] = accum_ref[...].astype(out_ref.dtype)


def project(start, blocks, halves, index, weight, final):
    rows, features = blocks[0].shape[1:]
    width = weight.shape[2]
    spans, begin = [], 0
    for block, half in zip(blocks, halves):
        spans.append((begin, block.shape[0], half))
        begin += block.shape[0]
    shape = (2, rows, width)

    def block_spec(begin, count):
        return pl.BlockSpec(
            (1, rows, features), lambda i, _: (jnp.clip(i - begin, 0, count - 1), 0, 0)
        )

    whole = lambda i, _: (0, 0, 0)
    return pl.pallas_call(
        functools.partial(project_kernel, spans, final),
        grid_spec=pltpu.PrefetchScalarGridSpec(
            num_scalar_prefetch=1,
            grid=(begin,),
            in_specs=[block_spec(at, count) for at, count, _ in spans]
            + [
                pl.BlockSpec((1, features, width), lambda i, index: (index[i], 0, 0)),
                pl.BlockSpec(start.shape, whole),
            ],
            out_specs=pl.BlockSpec(shape, whole),
            scratch_shapes=[pltpu.VMEM(shape, F32)],
        ),
        out_shape=jax.ShapeDtypeStruct(shape, BF16 if final else F32),
        compiler_params=pltpu.CompilerParams(vmem_limit_bytes=VMEM),
        cost_estimate=pl.CostEstimate(
            flops=2 * begin * rows * features * width,
            bytes_accessed=2 * begin * (rows + width) * features,
            transcendentals=0,
        ),
    )(index, *blocks, weight, start)


def kv_kernel(index_ref, rows_ref, key_ref, value_ref, keys_ref, values_ref):
    rows = rows_ref[0]
    keys_ref[0, 0] = jnp.dot(rows, key_ref[0], preferred_element_type=F32).astype(BF16)
    values_ref[0, 0] = jnp.dot(rows, value_ref[0], preferred_element_type=F32).astype(BF16)


def kv_partials(index, projected, kv_weight):
    _, rows, width = projected.shape
    out_shape = jax.ShapeDtypeStruct((SIDE, SIDE, rows, HEAD_DIM), BF16)
    return pl.pallas_call(
        kv_kernel,
        grid_spec=pltpu.PrefetchScalarGridSpec(
            num_scalar_prefetch=1,
            grid=(SIDE, SIDE),
            in_specs=[
                pl.BlockSpec((1, rows, width), lambda a, b, index: (index[a * SIDE + b] % 2, 0, 0)),
                pl.BlockSpec(
                    (1, width, HEAD_DIM), lambda a, b, index: (0, 0, index[a * SIDE + b] // 2)
                ),
                pl.BlockSpec(
                    (1, width, HEAD_DIM), lambda a, b, index: (1, 0, index[a * SIDE + b] // 2)
                ),
            ],
            out_specs=[
                pl.BlockSpec((1, 1, rows, HEAD_DIM), lambda a, b, _: (a, b, 0, 0)),
                pl.BlockSpec((1, 1, rows, HEAD_DIM), lambda a, b, _: (b, a, 0, 0)),
            ],
        ),
        out_shape=[out_shape, out_shape],
        compiler_params=pltpu.CompilerParams(vmem_limit_bytes=VMEM),
        cost_estimate=pl.CostEstimate(
            flops=2 * 32 * rows * width * HEAD_DIM,
            bytes_accessed=8 * 1024 * 1024,
            transcendentals=0,
        ),
    )(index, projected, kv_weight, kv_weight)


def query_kernel(full_ref, weight_ref, out_ref, inverse_ref, accum_ref):
    batch = out_ref.shape[0]
    step = pl.program_id(0)
    steps = pl.num_programs(0)

    @pl.when(step == 0)
    def _():
        total = jnp.zeros((batch, 1), F32)
        for rank in range(full_ref.shape[0]):
            hidden = full_ref[rank, :batch].astype(F32)
            total += jnp.sum(hidden * hidden, axis=1, keepdims=True)
        inverse_ref[...] = lax.rsqrt(total / D + 1e-05)
        accum_ref[...] = jnp.zeros_like(accum_ref)

    hidden = full_ref[step, :batch].astype(F32)
    gain = full_ref[step, batch : batch + 16].astype(F32)[:1]
    normed = (hidden * inverse_ref[...] * gain).astype(BF16)
    accum_ref[...] += jnp.dot(normed, weight_ref[...], preferred_element_type=F32)

    @pl.when(step == steps - 1)
    def _():
        out_ref[...] = accum_ref[...].astype(BF16)


def queries(full, query_weight, batch):
    ranks, rows, width = full.shape
    columns = query_weight.shape[1]
    return pl.pallas_call(
        query_kernel,
        grid=(ranks,),
        in_specs=[
            pl.BlockSpec((ranks, rows, width), lambda i: (0, 0, 0)),
            pl.BlockSpec((width, columns), lambda i: (i, 0)),
        ],
        out_specs=pl.BlockSpec((batch, columns), lambda i: (0, 0)),
        out_shape=jax.ShapeDtypeStruct((batch, columns), BF16),
        scratch_shapes=[pltpu.VMEM((batch, 1), F32), pltpu.VMEM((batch, columns), F32)],
        compiler_params=pltpu.CompilerParams(vmem_limit_bytes=VMEM),
        cost_estimate=pl.CostEstimate(
            flops=2 * batch * ranks * width * columns,
            bytes_accessed=12 * 1024 * 1024,
            transcendentals=0,
        ),
    )(full, query_weight)


def attend_kernel(
    index_ref, query_ref, kv_ref, row_ref, col_ref, weight_ref, first_ref, second_ref, context_ref
):
    batch, width = context_ref.shape

    @pl.when((pl.program_id(0) == 0) & (pl.program_id(1) == 0))
    def _():
        keys = kv_ref[:, :HEAD_DIM]
        values = kv_ref[:, HEAD_DIM:]
        allowed = row_ref[...] == col_ref[...]
        for head in range(width // HEAD_DIM):
            span = slice(head * HEAD_DIM, (head + 1) * HEAD_DIM)
            scores = lax.dot_general(
                query_ref[:, span], keys, (((1,), (1,)), ((), ())), preferred_element_type=F32
            ) * (1.0 / HEAD_DIM**0.5)
            scores = jnp.where(allowed, scores, -1e30)
            largest = jnp.max(scores, axis=1, keepdims=True)
            weights = jnp.where(allowed, jnp.exp(scores - largest), 0.0)
            total = jnp.sum(weights, axis=1, keepdims=True)
            summed = jnp.dot(weights.astype(BF16), values, preferred_element_type=F32)
            context_ref[:, span] = (summed / total).astype(BF16)

    branch = jnp.dot(context_ref[...], weight_ref[...], preferred_element_type=F32).astype(BF16)
    half = branch.shape[1] // 2
    first_ref[0, 0] = branch[:, :half]
    second_ref[0, 0] = branch[:, half:]


def attend(index, query, kv, row_request, col_request, out_weight):
    batch, width = query.shape
    rows = kv.shape[0]
    columns = out_weight.shape[1] // (SIDE * SIDE)
    half = columns // 2
    out_shape = jax.ShapeDtypeStruct((SIDE, SIDE, batch, half), BF16)
    fixed = lambda a, b, _: (0, 0)
    return pl.pallas_call(
        attend_kernel,
        grid_spec=pltpu.PrefetchScalarGridSpec(
            num_scalar_prefetch=1,
            grid=(SIDE, SIDE),
            in_specs=[
                pl.BlockSpec((batch, width), fixed),
                pl.BlockSpec((rows, 2 * HEAD_DIM), fixed),
                pl.BlockSpec((batch, 1), fixed),
                pl.BlockSpec((1, rows), fixed),
                pl.BlockSpec((width, columns), lambda a, b, index: (0, index[a * SIDE + b])),
            ],
            out_specs=[
                pl.BlockSpec((1, 1, batch, half), lambda a, b, _: (a, b, 0, 0)),
                pl.BlockSpec((1, 1, batch, half), lambda a, b, _: (b, a, 0, 0)),
            ],
            scratch_shapes=[pltpu.VMEM((batch, width), BF16)],
        ),
        out_shape=[out_shape, out_shape],
        compiler_params=pltpu.CompilerParams(vmem_limit_bytes=VMEM),
        cost_estimate=pl.CostEstimate(
            flops=2 * batch * width * out_weight.shape[1],
            bytes_accessed=12 * 1024 * 1024,
            transcendentals=batch * rows * 4,
        ),
    )(index, query, kv, row_request, col_request, out_weight)


def sum_phase(blocks, axis):
    arrived = [blocks[0]] + [shift(blocks[by], axis, by) for by in range(1, SIDE)]
    total = arrived[0].astype(F32)
    for block in arrived[1:]:
        total += block.astype(F32)
    return total


def gather_phase(block, axis):
    return [block] + [shift(block, axis, by) for by in (1, 3, 2)]


def forward_phase(stacked, axis):
    after = shift(stacked, axis, 1)
    before = shift(stacked, axis, 3)
    middle = stacked.shape[0] // 2
    return after, before, shift(after[:middle], axis, 1), shift(before[middle:], axis, 3)


def body(
    vision_rows,
    tile_count,
    tile_source,
    row_request,
    proj_weight,
    proj_bias,
    kv_weight,
    query_weight,
    out_weight,
    norm_gain,
    attn_gate,
    states,
):
    groups = lax.axis_size("group")
    ranks = lax.axis_size(TP)
    group = lax.axis_index("group")
    along_z = lax.axis_index(Z)
    along_x = lax.axis_index(X)
    tile_rows, features = vision_rows.shape[2:]
    per_group = vision_rows.shape[1] // groups
    slots = groups * per_group
    group_rows = slots * tile_rows
    half_rows = group_rows // 2
    req_grp = slots // MAXT
    batch = states.shape[1]
    width = states.shape[2]

    with jax.named_scope("gather_states"):
        local = states.reshape(STEPS * batch, width)
        gain_rows = jnp.broadcast_to(norm_gain[None, :], (16, width))
        full = lax.all_gather(jnp.concatenate([local, gain_rows], axis=0), TP)

    with jax.named_scope("gather_rows"):
        mine = vision_rows[0].reshape(groups, per_group, tile_rows, features)
        rows_a = gather_phase(mine[:, 0].reshape(half_rows, features), X)
        rows_b = gather_phase(mine[:, 1].reshape(half_rows, features), Z)
        stack_a = jnp.stack(rows_a)
        stack_b = jnp.stack(rows_b)
        far_a = forward_phase(stack_a, Z)
        far_b = forward_phase(stack_b, X)

    with jax.named_scope("project"):
        weight = proj_weight.reshape(ranks, features, proj_weight.shape[1])
        hops = jnp.array([0, 1, 3, 2], jnp.int32)

        def feature_blocks(z_hops, x_hops):
            return (along_z - z_hops) % SIDE * SIDE + (along_x - x_hops) % SIDE

        def both(far, chosen):
            return jnp.concatenate(
                [feature_blocks(far, chosen), feature_blocks(chosen, far)]
            ).astype(jnp.int32)

        start = proj_bias.astype(F32).reshape(1, 1, -1)
        accum = project(start, [stack_a, stack_b], (0, 1), both(0, hops), weight, False)
        accum = project(accum, [far_a[0], far_b[0]], (0, 1), both(1, hops), weight, False)
        accum = project(accum, [far_a[1], far_b[1]], (0, 1), both(3, hops), weight, False)
        projected = project(
            accum,
            [far_a[2], far_a[3], far_b[2], far_b[3]],
            (0, 0, 1, 1),
            both(2, hops),
            weight,
            True,
        )

    with jax.named_scope("kv"):
        steps = jnp.arange(SIDE, dtype=jnp.int32)
        targets = (along_z + steps[:, None]) % SIDE * SIDE + (along_x + steps[None, :]) % SIDE
        targets = targets.reshape(-1).astype(jnp.int32)
        part_keys, part_values = kv_partials(targets, projected, kv_weight)
        keys = sum_phase(part_keys, Z).astype(BF16)
        values = sum_phase(part_values, X).astype(BF16)
        keys = sum_phase(keys, X).astype(BF16)
        values = sum_phase(values, Z).astype(BF16)
        kv = jnp.concatenate([keys, values], axis=1)
        kv = kv.reshape(groups, 1, tile_rows, 2 * HEAD_DIM)
        kv = jnp.broadcast_to(kv, (groups, 2, tile_rows, 2 * HEAD_DIM))
        kv = kv.reshape(slots, tile_rows, 2 * HEAD_DIM)
        kv = lax.all_to_all(kv, ("group", "pr"), 0, 0)
        kv = kv.reshape(group_rows, 2 * HEAD_DIM)

    with jax.named_scope("query"):
        query = queries(full, query_weight, STEPS * batch)

    with jax.named_scope("mask"):
        sources = lax.dynamic_index_in_dim(tile_source, group, 0, keepdims=False)
        counts = lax.dynamic_slice_in_dim(tile_count, group * req_grp, req_grp, 0)
        places = jnp.arange(slots, dtype=jnp.int32)
        request = places // MAXT
        valid = places % MAXT < jnp.repeat(counts, MAXT)
        label = jnp.where(valid, request, -1)
        hits = sources[None, :] == places[:, None]
        tile_label = jnp.sum(jnp.where(hits, label[None, :], 0), axis=1)
        col_request = jnp.repeat(tile_label, tile_rows)[None, :]
        rows = jnp.concatenate([row_request[0]] * STEPS)[:, None]

    with jax.named_scope("attend"):
        first, second = attend(targets, query, kv, rows, col_request, out_weight)

    with jax.named_scope("mix"):
        first = sum_phase(first, Z).astype(BF16)
        second = sum_phase(second, X).astype(BF16)
        first = sum_phase(first, X)
        second = sum_phase(second, Z)
        reduced = jnp.concatenate([first, second], axis=1)
        mixed = local.astype(F32) + jnp.tanh(attn_gate) * reduced
        return mixed.astype(BF16).reshape(STEPS, batch, width)


def solution(mesh):
    groups = mesh.shape["group"]
    split = Mesh(mesh.devices.reshape(groups, SIDE, 2, 2), ("group",) + TP)
    in_specs = (
        P("group", None, None, TP),
        P(),
        P(),
        P("group", None),
        P(None, TP),
        P(TP),
        P(None, TP, None),
        P(None, TP),
        P(TP, None),
        P(TP),
        P(),
        P(None, "group", TP),
    )
    out_specs = P(None, "group", TP)
    return jax.shard_map(body, mesh=split, in_specs=in_specs, out_specs=out_specs, check_vma=False)
```

```python
import functools

import jax
import jax.numpy as jnp
from jax import lax
from jax.experimental import pallas as pl
from jax.experimental.pallas import tpu as pltpu
from jax.sharding import Mesh, PartitionSpec as P

D = 8192
HEADS = 64
KV_HEADS = 8
HEAD_DIM = 128
MAXT = 4
STEPS = 2
SIDE = 4
F32 = jnp.float32
BF16 = jnp.bfloat16
TP = ("z", "xh", "pr")
EVERY = ("group",) + TP
FIRST, SECOND = 0, 1
VMEM = 58 * 1024 * 1024


def place(core, first, second):
    return jnp.where(core == 0, second * SIDE + first, first * SIDE + second)


def shift(value, groups, order, by):
    pairs = []
    for group in range(groups):
        for z in range(SIDE):
            for x in range(SIDE):
                if group % 2 == order:
                    other = z * SIDE + (x + by) % SIDE
                else:
                    other = (z + by) % SIDE * SIDE + x
                base = group * SIDE * SIDE
                pairs.append((base + z * SIDE + x, base + other))
    return lax.ppermute(value, EVERY, pairs)


def project_kernel(spans, index_ref, *refs):
    blocks = refs[: len(spans)]
    weight_ref, start_ref, out_ref, accum_ref = refs[len(spans) :]
    step = pl.program_id(0)

    @pl.when(step == 0)
    def _():
        accum_ref[...] = jnp.broadcast_to(start_ref[...], accum_ref.shape)

    for block, (begin, count) in zip(blocks, spans):

        @pl.when((step >= begin) & (step < begin + count))
        def _():
            accum_ref[...] += lax.dot_general(
                block[0], weight_ref[0], (((0,), (0,)), ((), ())), preferred_element_type=F32
            )

    @pl.when(step == pl.num_programs(0) - 1)
    def _():
        out_ref[...] = accum_ref[...].astype(out_ref.dtype)


def project(start, blocks, index, weight, kind):
    features, rows = blocks[0].shape[1:]
    width = weight.shape[2]
    spans, begin = [], 0
    for block in blocks:
        spans.append((begin, block.shape[0]))
        begin += block.shape[0]
    shape = (rows, width)

    def block_spec(begin, count):
        return pl.BlockSpec(
            (1, features, rows), lambda i, _: (jnp.clip(i - begin, 0, count - 1), 0, 0)
        )

    return pl.pallas_call(
        functools.partial(project_kernel, spans),
        grid_spec=pltpu.PrefetchScalarGridSpec(
            num_scalar_prefetch=1,
            grid=(begin,),
            in_specs=[block_spec(at, count) for at, count in spans]
            + [
                pl.BlockSpec((1, features, width), lambda i, index: (index[i], 0, 0)),
                pl.BlockSpec(start.shape, lambda i, _: (0, 0)),
            ],
            out_specs=pl.BlockSpec(shape, lambda i, _: (0, 0)),
            scratch_shapes=[pltpu.VMEM(shape, F32)],
        ),
        out_shape=jax.ShapeDtypeStruct(shape, kind),
        compiler_params=pltpu.CompilerParams(vmem_limit_bytes=VMEM),
        cost_estimate=pl.CostEstimate(
            flops=2 * begin * rows * features * width,
            bytes_accessed=2 * begin * (rows + width) * features,
            transcendentals=0,
        ),
    )(index, *blocks, weight, start)


def kv_kernel(place_ref, rows_ref, weight_ref, out_ref):
    half = out_ref.shape[2]
    for head in range(KV_HEADS):
        span = slice(head * HEAD_DIM, (head + 1) * HEAD_DIM)
        weight = jnp.concatenate([weight_ref[0, :, span], weight_ref[1, :, span]], axis=1)
        part = jnp.dot(rows_ref[...], weight, preferred_element_type=F32).astype(BF16)
        for parity in range(2):
            at = place_ref[2 * head + parity]
            out_ref[at // SIDE, at % SIDE] = part[parity * half : (parity + 1) * half]


def kv_partials(places, projected, kv_weight):
    rows, width = projected.shape
    vmem = pl.BlockSpec(memory_space=pltpu.VMEM)
    return pl.pallas_call(
        kv_kernel,
        in_specs=[pl.BlockSpec(memory_space=pltpu.SMEM), vmem, vmem],
        out_specs=vmem,
        out_shape=jax.ShapeDtypeStruct((SIDE, SIDE, rows // 2, 2 * HEAD_DIM), BF16),
        compiler_params=pltpu.CompilerParams(vmem_limit_bytes=VMEM),
        cost_estimate=pl.CostEstimate(
            flops=2 * rows * width * 2 * KV_HEADS * HEAD_DIM,
            bytes_accessed=5 * 1024 * 1024,
            transcendentals=0,
        ),
    )(places, projected, kv_weight)


def query_kernel(full_ref, weight_ref, out_ref, inverse_ref, accum_ref):
    batch = out_ref.shape[0]
    width = full_ref.shape[2]
    part = weight_ref.shape[0] // width
    step = pl.program_id(0)

    @pl.when(step == 0)
    def _():
        total = jnp.zeros((batch, 1), F32)
        for rank in range(full_ref.shape[0]):
            hidden = full_ref[rank, :batch].astype(F32)
            total += jnp.sum(hidden * hidden, axis=1, keepdims=True)
        inverse_ref[...] = lax.rsqrt(total / D + 1e-05)
        accum_ref[...] = jnp.zeros_like(accum_ref)

    for inner in range(part):
        rank = step * part + inner
        hidden = full_ref[rank, :batch].astype(F32)
        gain = full_ref[rank, batch : batch + 16].astype(F32)[:1]
        normed = (hidden * inverse_ref[...] * gain).astype(BF16)
        span = slice(inner * width, (inner + 1) * width)
        accum_ref[...] += jnp.dot(normed, weight_ref[span, :], preferred_element_type=F32)

    @pl.when(step == pl.num_programs(0) - 1)
    def _():
        out_ref[...] = accum_ref[...].astype(BF16)


def queries(full, query_weight, batch):
    ranks, rows, width = full.shape
    columns = query_weight.shape[1]
    return pl.pallas_call(
        query_kernel,
        grid=(ranks // 4,),
        in_specs=[
            pl.BlockSpec((ranks, rows, width), lambda i: (0, 0, 0)),
            pl.BlockSpec((4 * width, columns), lambda i: (i, 0)),
        ],
        out_specs=pl.BlockSpec((batch, columns), lambda i: (0, 0)),
        out_shape=jax.ShapeDtypeStruct((batch, columns), BF16),
        scratch_shapes=[pltpu.VMEM((batch, 1), F32), pltpu.VMEM((batch, columns), F32)],
        compiler_params=pltpu.CompilerParams(vmem_limit_bytes=VMEM),
        cost_estimate=pl.CostEstimate(
            flops=2 * batch * ranks * width * columns,
            bytes_accessed=12 * 1024 * 1024,
            transcendentals=0,
        ),
    )(full, query_weight)


def attend_kernel(
    place_ref, query_ref, kv_ref, row_ref, col_ref, weight_ref, out_ref, context_ref
):
    batch, width = context_ref.shape
    columns = out_ref.shape[3]
    part = weight_ref.shape[1] // columns
    step = pl.program_id(0)

    @pl.when(step == 0)
    def _():
        keys = kv_ref[:, :HEAD_DIM]
        values = kv_ref[:, HEAD_DIM:]
        allowed = row_ref[...] == col_ref[...]
        for head in range(width // HEAD_DIM):
            span = slice(head * HEAD_DIM, (head + 1) * HEAD_DIM)
            scores = lax.dot_general(
                query_ref[:, span], keys, (((1,), (1,)), ((), ())), preferred_element_type=F32
            ) * (1.0 / HEAD_DIM**0.5)
            scores = jnp.where(allowed, scores, -1e30)
            largest = jnp.max(scores, axis=1, keepdims=True)
            weights = jnp.where(allowed, jnp.exp(scores - largest), 0.0)
            total = jnp.sum(weights, axis=1, keepdims=True)
            summed = jnp.dot(weights.astype(BF16), values, preferred_element_type=F32)
            context_ref[:, span] = (summed / total).astype(BF16)

    for inner in range(part):
        span = slice(inner * columns, (inner + 1) * columns)
        branch = jnp.dot(context_ref[...], weight_ref[:, span], preferred_element_type=F32)
        at = place_ref[step * part + inner]
        out_ref[at // SIDE, at % SIDE] = branch.astype(BF16)


def attend(places, query, kv, row_request, col_request, out_weight):
    batch, width = query.shape
    rows = kv.shape[0]
    columns = out_weight.shape[1] // (SIDE * SIDE)
    shape = (SIDE, SIDE, batch, columns)
    fixed = lambda i, _: (0, 0)
    return pl.pallas_call(
        attend_kernel,
        grid_spec=pltpu.PrefetchScalarGridSpec(
            num_scalar_prefetch=1,
            grid=(SIDE,),
            in_specs=[
                pl.BlockSpec((batch, width), fixed),
                pl.BlockSpec((rows, 2 * HEAD_DIM), fixed),
                pl.BlockSpec((batch, 1), fixed),
                pl.BlockSpec((1, rows), fixed),
                pl.BlockSpec((width, SIDE * columns), lambda i, _: (0, i)),
            ],
            out_specs=pl.BlockSpec(shape, lambda i, _: (0, 0, 0, 0)),
            scratch_shapes=[pltpu.VMEM((batch, width), BF16)],
        ),
        out_shape=jax.ShapeDtypeStruct(shape, BF16),
        compiler_params=pltpu.CompilerParams(vmem_limit_bytes=VMEM),
        cost_estimate=pl.CostEstimate(
            flops=2 * batch * width * out_weight.shape[1],
            bytes_accessed=12 * 1024 * 1024,
            transcendentals=batch * rows * 4,
        ),
    )(places, query, kv, row_request, col_request, out_weight)


def sum_phase(blocks, groups, order):
    total = blocks[0].astype(F32)
    for by in (1, 3, 2):
        total += shift(blocks[by], groups, order, by).astype(F32)
    return total


def body(
    vision_rows,
    tile_count,
    tile_source,
    row_request,
    proj_weight,
    proj_bias,
    kv_weight,
    query_weight,
    out_weight,
    norm_gain,
    attn_gate,
    states,
):
    groups = lax.axis_size("group")
    ranks = lax.axis_size(TP)
    group = lax.axis_index("group")
    along_z = lax.axis_index("z")
    along_x = lax.axis_index(("xh", "pr"))
    core = group % 2
    first = jnp.where(core == 0, along_x, along_z)
    second = jnp.where(core == 0, along_z, along_x)
    tile_rows, features = vision_rows.shape[2:]
    per_group = vision_rows.shape[1] // groups
    slots = groups * per_group
    group_rows = slots * tile_rows
    req_grp = slots // MAXT
    batch = states.shape[1]
    width = states.shape[2]

    with jax.named_scope("gather_rows"):
        mine = vision_rows[0].reshape(groups, per_group, tile_rows, features)
        mine = mine.transpose(3, 1, 0, 2).reshape(1, features, group_rows)
        near = [mine] + [shift(mine, groups, FIRST, by) for by in (1, 3, 2)]
        near = jnp.concatenate(near)
        after = shift(near, groups, SECOND, 1)
        before = shift(near, groups, SECOND, 3)

    with jax.named_scope("gather_states"):
        local = states.reshape(STEPS * batch, width)
        gain_rows = jnp.broadcast_to(norm_gain[None, :], (16, width))
        full = lax.all_gather(jnp.concatenate([local, gain_rows], axis=0), TP)

    with jax.named_scope("project"):
        weight = proj_weight.reshape(ranks, features, proj_weight.shape[1])
        hops = jnp.array([0, 1, 3, 2], jnp.int32)

        def index(far):
            return place(core, (first - hops) % SIDE, (second - far) % SIDE).astype(jnp.int32)

        bias = proj_bias.astype(F32)[None, :]
        accum = project(bias, [near], index(0), weight, F32)
        after, before, accum = lax.optimization_barrier((after, before, accum))

    with jax.named_scope("gather_rows"):
        across_after = shift(after[:2], groups, SECOND, 1)
        across_before = shift(before[2:], groups, SECOND, 3)

    with jax.named_scope("project"):
        accum = project(accum, [after], index(1), weight, F32)
        accum = project(accum, [before], index(3), weight, F32)
        projected = project(accum, [across_after, across_before], index(2), weight, BF16)

    with jax.named_scope("kv"):
        rank = jnp.arange(ranks, dtype=jnp.int32)
        of_x, of_z = rank % SIDE, rank // SIDE
        to_first = (jnp.where(core == 0, of_x, of_z) - first) % SIDE
        to_second = (jnp.where(core == 0, of_z, of_x) - second) % SIDE
        places = (to_first * SIDE + to_second).astype(jnp.int32)
        kv = kv_partials(places, projected, kv_weight)
        kv = sum_phase(kv, groups, FIRST).astype(BF16)
        kv = sum_phase(kv, groups, SECOND).astype(BF16)
        kv = kv.reshape(groups, 1, tile_rows, 2 * HEAD_DIM)
        kv = jnp.broadcast_to(kv, (groups, 2, tile_rows, 2 * HEAD_DIM))
        kv = kv.reshape(slots, tile_rows, 2 * HEAD_DIM)
        kv = lax.all_to_all(kv, ("group", "pr"), 0, 0)
        kv = kv.reshape(group_rows, 2 * HEAD_DIM)

    with jax.named_scope("query"):
        query = queries(full, query_weight, STEPS * batch)

    with jax.named_scope("mask"):
        sources = lax.dynamic_index_in_dim(tile_source, group, 0, keepdims=False)
        counts = lax.dynamic_slice_in_dim(tile_count, group * req_grp, req_grp, 0)
        spots = jnp.arange(slots, dtype=jnp.int32)
        request = spots // MAXT
        valid = spots % MAXT < jnp.repeat(counts, MAXT)
        label = jnp.where(valid, request, -1)
        hits = sources[None, :] == spots[:, None]
        tile_label = jnp.sum(jnp.where(hits, label[None, :], 0), axis=1)
        col_request = jnp.repeat(tile_label, tile_rows)[None, :]
        rows = jnp.concatenate([row_request[0]] * STEPS)[:, None]

    with jax.named_scope("attend"):
        branch = attend(places, query, kv, rows, col_request, out_weight)

    with jax.named_scope("mix"):
        branch = sum_phase(branch, groups, FIRST).astype(BF16)
        reduced = sum_phase(branch, groups, SECOND)
        mixed = local.astype(F32) + jnp.tanh(attn_gate) * reduced
        return mixed.astype(BF16).reshape(STEPS, batch, width)


def solution(mesh):
    groups = mesh.shape["group"]
    split = Mesh(mesh.devices.reshape(groups, SIDE, 2, 2), ("group",) + TP)
    in_specs = (
        P("group", None, None, TP),
        P(),
        P(),
        P("group", None),
        P(None, TP),
        P(TP),
        P(None, TP, None),
        P(None, TP),
        P(TP, None),
        P(TP),
        P(),
        P(None, "group", TP),
    )
    out_specs = P(None, "group", TP)
    return jax.shard_map(body, mesh=split, in_specs=in_specs, out_specs=out_specs, check_vma=False)
```

```python
import functools

import jax
import jax.numpy as jnp
from jax import lax
from jax.experimental import pallas as pl
from jax.experimental.pallas import tpu as pltpu
from jax.sharding import Mesh, PartitionSpec as P

D = 8192
KV_HEADS = 8
HEAD_DIM = 128
MAXT = 4
STEPS = 2
SIDE = 4
F32 = jnp.float32
BF16 = jnp.bfloat16
TP = ("z", "xh", "pr")
X = ("xh", "pr")
Z = "z"
EVERY = ("group",) + TP
FIRST, SECOND = 0, 1
HOPS = (0, 1, 3, 2)
GRANT = 16 * 1024 * 1024
ANY = pl.BlockSpec(memory_space=pl.ANY)
IN_HBM = pl.BlockSpec(memory_space=pltpu.HBM)
IN_VMEM = pl.BlockSpec(memory_space=pltpu.VMEM)
IN_SMEM = pl.BlockSpec(memory_space=pltpu.SMEM)


def along(value, axis, by):
    return lax.ppermute(value, axis, [(i, (i + by) % SIDE) for i in range(SIDE)])


def shift(value, groups, order, by):
    pairs = []
    for group in range(groups):
        for z in range(SIDE):
            for x in range(SIDE):
                if group % 2 == order:
                    other = z * SIDE + (x + by) % SIDE
                else:
                    other = (z + by) % SIDE * SIDE + x
                base = group * SIDE * SIDE
                pairs.append((base + z * SIDE + x, base + other))
    return lax.ppermute(value, EVERY, pairs)


def in_hbm(value):
    return pltpu.with_memory_space_constraint(value, pltpu.HBM)


def in_vmem(value):
    return pltpu.with_memory_space_constraint(value, pltpu.VMEM)


def kernel_call(kernel, operands, specs, out, scratch=(), flops=0, moved=0, transcendentals=0):
    return pl.pallas_call(
        kernel,
        in_specs=specs,
        out_specs=jax.tree.map(lambda _: IN_VMEM, out),
        out_shape=out,
        scratch_shapes=list(scratch),
        compiler_params=pltpu.CompilerParams(vmem_limit_bytes=GRANT),
        cost_estimate=pl.CostEstimate(
            flops=flops, bytes_accessed=moved, transcendentals=transcendentals
        ),
    )(*operands)


def wrap(value):
    return lax.rem(value + SIDE, SIDE)


def position():
    z = lax.axis_index("z")
    x = lax.axis_index("xh") * 2 + lax.axis_index("pr")
    return z, x, lax.rem(lax.axis_index("group"), 2)


def rank_from_here(first_by, second_by):
    z, x, core = position()
    first = jnp.where(core == 0, x, z)
    second = jnp.where(core == 0, z, x)
    first, second = wrap(first + first_by), wrap(second + second_by)
    return jnp.where(core == 0, second * SIDE + first, first * SIDE + second)


def rank_by_hops(z_hops, x_hops):
    z, x, _ = position()
    return wrap(z - z_hops) * SIDE + wrap(x - x_hops)


def join_kernel(moves, *refs):
    copies = []
    sem = refs[-1]
    for at, (source, low, target, first, count) in enumerate(moves):
        copies.append(
            pltpu.make_async_copy(
                refs[source].at[pl.ds(low, count)], refs[target].at[pl.ds(first, count)], sem.at[at]
            )
        )
    for copy in copies:
        copy.start()
    for copy in copies:
        copy.wait()


def join(arrays, moves, shapes, after=()):
    offset = len(arrays) + len(after)
    moves = [(a, low, offset + b, first, count) for a, low, b, first, count in moves]
    moved = 4 * sum(a.size for a in arrays)
    return kernel_call(
        functools.partial(join_kernel, moves),
        [*arrays, *after],
        [ANY] * offset,
        [pltpu.VMEM(shape, BF16) for shape in shapes],
        [pltpu.SemaphoreType.DMA((len(moves),))],
        moved=moved,
    )


def load_kernel(*refs):
    count = len(refs) // 3
    copies = [
        pltpu.make_async_copy(refs[i], refs[count + i], refs[2 * count + i]) for i in range(count)
    ]
    for copy in copies:
        copy.start()
    for copy in copies:
        copy.wait()


def load(*values):
    return kernel_call(
        load_kernel,
        [in_hbm(value) for value in values],
        [IN_HBM] * len(values),
        [pltpu.VMEM(value.shape, value.dtype) for value in values],
        [pltpu.SemaphoreType.DMA(()) for _ in values],
        moved=4 * sum(value.size for value in values),
    )


def add_products(sums, blocks, weight_ref):
    for ref, half, origins in blocks:
        for inner, hops in enumerate(origins):
            sums[half] = sums[half] + lax.dot_general(
                ref[inner],
                weight_ref[rank_by_hops(*hops)],
                (((0,), (0,)), ((), ())),
                preferred_element_type=F32,
            )


def project_kernel(parts, *refs):
    blocks = [(ref, *part) for ref, part in zip(refs, parts)]
    weight_ref, start_ref, out_ref, token_ref = refs[len(parts) : len(parts) + 4]
    if len(start_ref.shape) == 3:
        sums = [start_ref[0], start_ref[1]]
    else:
        rows = blocks[0][0].shape[2]
        bias = jnp.broadcast_to(start_ref[...].astype(F32), (rows, start_ref.shape[1]))
        sums = [bias, bias]
    add_products(sums, blocks, weight_ref)
    for half in range(2):
        out_ref[half] = sums[half]
    token_ref[...] = jnp.zeros_like(token_ref)


def project(start, blocks, parts, weight):
    features, rows = blocks[0].shape[1:]
    width = weight.shape[2]
    count = sum(block.shape[0] for block in blocks)
    return kernel_call(
        functools.partial(project_kernel, parts),
        [*map(in_vmem, blocks), in_vmem(weight), start],
        [IN_VMEM] * (len(blocks) + 2),
        [pltpu.VMEM((2, rows, width), F32), jax.ShapeDtypeStruct((8, 128), F32)],
        flops=2 * count * rows * features * width,
        moved=2 * count * (rows + width) * features,
    )


def kv_kernel(parts, tokens, *refs):
    blocks = [(ref, *part) for ref, part in zip(refs, parts)]
    weight_ref, kv_weight_ref, start_ref = refs[len(parts) : len(parts) + 3]
    outs = refs[len(parts) + 3 + tokens : -1]
    rows_ref = refs[-1]
    sums = [start_ref[0], start_ref[1]]
    add_products(sums, blocks, weight_ref)
    half_rows = sums[0].shape[0]
    for half in range(2):
        rows_ref[half] = sums[half].astype(BF16)
    for first_by in range(SIDE):
        for second_by in range(SIDE):
            rank = rank_from_here(first_by, second_by)
            span = pl.ds(pl.multiple_of(rank // 2 * HEAD_DIM, HEAD_DIM), HEAD_DIM)
            weight = jnp.concatenate([kv_weight_ref[0, :, span], kv_weight_ref[1, :, span]], axis=1)
            outs[first_by][second_by] = jnp.dot(
                rows_ref[lax.rem(rank, 2)], weight, preferred_element_type=F32
            ).astype(BF16)


def kv_partials(start, blocks, parts, weight, kv_weight, after):
    _, rows, width = start.shape
    return kernel_call(
        functools.partial(kv_kernel, parts, len(after)),
        [*map(in_vmem, blocks), in_vmem(weight), in_vmem(kv_weight), start, *after],
        [IN_VMEM] * (len(blocks) + 3) + [ANY] * len(after),
        [pltpu.VMEM((SIDE, rows, 2 * HEAD_DIM), BF16) for _ in range(SIDE)],
        [pltpu.VMEM((2, rows, width), BF16)],
        flops=4 * rows * width * 2 * KV_HEADS * HEAD_DIM,
        moved=8 * 1024 * 1024,
    )


def sum_kernel(copies, tokens, *refs):
    sources, outs = refs[:SIDE], refs[SIDE + tokens :]
    for at in range(sources[0].shape[0]):
        total = sources[0][at].astype(F32)
        for source in sources[1:]:
            total = total + source[at].astype(F32)
        total = total.astype(BF16)
        if copies == 1:
            outs[at][...] = total
        else:
            for twin in range(copies):
                outs[0][copies * at + twin] = total


def sum_blocks(sources, copies=1, after=()):
    count, rows, width = sources[0].shape
    if copies == 1:
        out = [pltpu.VMEM((rows, width), BF16) for _ in range(count)]
    else:
        out = [jax.ShapeDtypeStruct((count * copies, rows, width), BF16)]
    return kernel_call(
        functools.partial(sum_kernel, copies, len(after)),
        [*map(in_vmem, sources), *after],
        [IN_VMEM] * SIDE + [ANY] * len(after),
        out,
        flops=SIDE * sources[0].size,
        moved=10 * sources[0].size,
    )


def query_kernel(batch, *refs):
    parts, (weight_ref, out_ref, buffer, sem) = refs[:SIDE], refs[SIDE:]
    pieces = sem.shape[0]
    deep = buffer.shape[0] // pieces
    copies = [
        pltpu.make_async_copy(
            weight_ref.at[pl.ds(i * deep, deep)], buffer.at[pl.ds(i * deep, deep)], sem.at[i]
        )
        for i in range(pieces)
    ]
    for copy in copies:
        copy.start()
    total = jnp.zeros((batch, 1), F32)
    for part in parts:
        for block in range(SIDE):
            hidden = part[block, :batch, :].astype(F32)
            total += jnp.sum(hidden * hidden, axis=1, keepdims=True)
    inverse = lax.rsqrt(total / D + 1e-05)
    for copy in copies:
        copy.wait()
    accum = jnp.zeros(out_ref.shape, F32)
    for part, far in zip(parts, HOPS):
        width = part.shape[2]
        for block, near in enumerate(HOPS):
            hidden = part[block, :batch, :].astype(F32)
            gain = part[block, batch : batch + 16, :].astype(F32)[:1]
            normed = (hidden * inverse * gain).astype(BF16)
            rank = rank_from_here(-far, -near)
            rows = pl.ds(pl.multiple_of(rank * width, width), width)
            accum += jnp.dot(normed, buffer[rows, :], preferred_element_type=F32)
    out_ref[...] = accum.astype(BF16)


def queries(parts, query_weight, batch):
    columns = query_weight.shape[1]
    return kernel_call(
        functools.partial(query_kernel, batch),
        [*parts, in_hbm(query_weight)],
        [IN_VMEM] * SIDE + [IN_HBM],
        jax.ShapeDtypeStruct((batch, columns), BF16),
        [pltpu.VMEM(query_weight.shape, BF16), pltpu.SemaphoreType.DMA((8,))],
        flops=2 * batch * D * columns,
        moved=12 * 1024 * 1024,
    )


def attend_kernel(
    source_ref, count_ref, request_ref, query_ref, kv_ref, weight_ref, *refs
):
    outs, (buffer, sem) = refs[:SIDE], refs[SIDE:]
    batch, width = query_ref.shape
    columns = outs[0].shape[2]
    slots, tile_rows, both = kv_ref.shape
    rows = slots * tile_rows
    group = lax.axis_index("group")
    pieces = sem.shape[0]
    wide = buffer.shape[1] // pieces
    copies = []
    for first_by in range(SIDE):
        for second_by in range(SIDE):
            at = first_by * SIDE + second_by
            span = pl.ds(pl.multiple_of(rank_from_here(first_by, second_by) * wide, wide), wide)
            copies.append(
                pltpu.make_async_copy(
                    weight_ref.at[:, span], buffer.at[:, pl.ds(at * wide, wide)], sem.at[at]
                )
            )
    for copy in copies[:4]:
        copy.start()

    tile = lax.broadcasted_iota(jnp.int32, (1, rows), 1) // tile_rows
    owner = jnp.full((1, rows), -1, jnp.int32)
    for place in range(slots):
        request = place // MAXT
        valid = place % MAXT < count_ref[group * (slots // MAXT) + request]
        label = jnp.where(valid, request, -1)
        owner = jnp.where(tile == source_ref[group, place], label, owner)
    per_step = request_ref.shape[1]
    here = lax.broadcasted_iota(jnp.int32, (per_step, per_step), 0)
    there = lax.broadcasted_iota(jnp.int32, (per_step, per_step), 1)
    asked = jnp.where(here == there, request_ref[...], 0)
    asked = jnp.sum(asked, axis=1, keepdims=True)
    allowed = jnp.concatenate([asked] * (batch // per_step), axis=0) == owner

    kv = kv_ref[...].reshape(rows, both)
    keys, values = kv[:, :HEAD_DIM], kv[:, HEAD_DIM:]
    contexts = []
    for head in range(width // HEAD_DIM):
        for copy in copies[4 + 2 * head : 6 + 2 * head]:
            copy.start()
        span = slice(head * HEAD_DIM, (head + 1) * HEAD_DIM)
        scores = lax.dot_general(
            query_ref[:, span], keys, (((1,), (1,)), ((), ())), preferred_element_type=F32
        ) * (1.0 / HEAD_DIM**0.5)
        scores = jnp.where(allowed, scores, -1e30)
        largest = jnp.max(scores, axis=1, keepdims=True)
        weights = jnp.where(allowed, jnp.exp(scores - largest), 0.0)
        total = jnp.sum(weights, axis=1, keepdims=True)
        summed = jnp.dot(weights.astype(BF16), values, preferred_element_type=F32)
        contexts.append((summed / total).astype(BF16))
    for copy in copies[4 + 2 * len(contexts) :]:
        copy.start()
    context = jnp.concatenate(contexts, axis=1)
    for first_by in range(SIDE):
        for second_by in range(SIDE):
            at = first_by * SIDE + second_by
            copies[at].wait()
            branch = jnp.dot(
                context, buffer[:, at * wide : (at + 1) * wide], preferred_element_type=F32
            )
            outs[first_by][second_by] = branch.astype(BF16)


def attend(tile_source, tile_count, row_request, query, kv, out_weight):
    batch, width = query.shape
    ranks = SIDE * SIDE
    columns = out_weight.shape[1] // ranks
    return kernel_call(
        attend_kernel,
        [tile_source, tile_count, row_request, query, kv, in_hbm(out_weight)],
        [IN_SMEM, IN_SMEM, IN_VMEM, IN_VMEM, IN_VMEM, IN_HBM],
        [pltpu.VMEM((SIDE, batch, columns), BF16) for _ in range(SIDE)],
        [pltpu.VMEM(out_weight.shape, BF16), pltpu.SemaphoreType.DMA((ranks,))],
        flops=2 * batch * width * out_weight.shape[1],
        moved=12 * 1024 * 1024,
        transcendentals=batch * 4 * 512,
    )


def mix_kernel(gate_ref, local_ref, *refs):
    sources, out_ref = refs[:SIDE], refs[SIDE]
    steps, batch, width = local_ref.shape
    gate = jnp.tanh(jnp.full((1, width), gate_ref[0, 0], F32))
    for step in range(steps):
        span = slice(step * batch, (step + 1) * batch)
        total = sources[0][span].astype(F32)
        for source in sources[1:]:
            total = total + source[span].astype(F32)
        out_ref[step] = (local_ref[step].astype(F32) + gate * total).astype(BF16)


def mix(gate, local, sources):
    return kernel_call(
        mix_kernel,
        [gate.reshape(1, 1), local, *map(in_vmem, sources)],
        [IN_SMEM, IN_VMEM] + [IN_VMEM] * SIDE,
        jax.ShapeDtypeStruct(local.shape, BF16),
        flops=SIDE * local.size,
        moved=12 * local.size,
    )


def body(
    vision_rows,
    tile_count,
    tile_source,
    row_request,
    proj_weight,
    proj_bias,
    kv_weight,
    query_weight,
    out_weight,
    norm_gain,
    attn_gate,
    states,
):
    groups = lax.axis_size("group")
    ranks = lax.axis_size(TP)
    tile_rows, features = vision_rows.shape[2:]
    per_group = vision_rows.shape[1] // groups
    half_rows = groups * tile_rows
    batch = STEPS * states.shape[1]
    width = states.shape[2]
    height = batch + 16
    block = (features, half_rows)

    with jax.named_scope("gather_rows"):
        mine = vision_rows[0].reshape(groups, per_group, tile_rows, features)
        mine = mine.transpose(1, 3, 0, 2).reshape(per_group, 1, *block)
        near_a = [mine[0]] + [along(mine[0], X, by) for by in HOPS[1:]]
        near_b = [mine[1]] + [along(mine[1], Z, by) for by in HOPS[1:]]
        near_a, near_b = join(
            near_a + near_b,
            [(i, 0, i // SIDE, i % SIDE, 1) for i in range(2 * SIDE)],
            [(SIDE, *block)] * 2,
        )
        far = [along(near_a, Z, 1), along(near_a, Z, 3), along(near_b, X, 1), along(near_b, X, 3)]

    with jax.named_scope("project"):
        weight, kv_here = load(proj_weight.reshape(ranks, *block[:1], -1), kv_weight)

        def origins(across, chosen=HOPS):
            return (0, [(across, hop) for hop in chosen]), (1, [(hop, across) for hop in chosen])

        accum, token = project(proj_bias[None, :], [near_a, near_b], origins(0), weight)

    with jax.named_scope("gather_states"):
        gain_rows = jnp.broadcast_to(norm_gain[None, :], (16, width))
        (carried,) = join(
            [states.reshape(batch, width), gain_rows],
            [(0, 0, 0, 0, batch), (1, 0, 0, batch, 16)],
            [(height, width)],
            [token],
        )
        carried = carried.reshape(1, height, width)
        arrived = [shift(carried, groups, SECOND, by) for by in HOPS[1:]]

    with jax.named_scope("gather_rows"):
        cut = join(
            far,
            [(i, i % 2 * 2, i, 0, 2) for i in range(4)],
            [(2, *block)] * 4,
            [token],
        )
        last = [along(cut[0], Z, 1), along(cut[1], Z, 3), along(cut[2], X, 1), along(cut[3], X, 3)]

    with jax.named_scope("project"):
        accum, _ = project(accum, [far[0], far[2]], origins(1), weight)
        accum, _ = project(accum, [far[1], far[3]], origins(3), weight)
        low_a, low_b = origins(2, HOPS[:2])
        high_a, high_b = origins(2, HOPS[2:])
        kv = kv_partials(accum, last, (low_a, high_a, low_b, high_b), weight, kv_here, arrived)

    with jax.named_scope("gather_states"):
        (states_near,) = join(
            [carried] + arrived,
            [(i, 0, 0, i, 1) for i in range(SIDE)],
            [(SIDE, height, width)],
        )
        states_all = [states_near] + [shift(states_near, groups, FIRST, by) for by in HOPS[1:]]

    with jax.named_scope("kv"):
        kv = [kv[0]] + [shift(kv[by], groups, FIRST, by) for by in HOPS[1:]]
        kv = sum_blocks(kv, after=states_all[1:])
        kv = [kv[0]] + [shift(kv[by], groups, SECOND, by) for by in HOPS[1:]]
        kv = [part.reshape(groups, tile_rows, 2 * HEAD_DIM) for part in kv]
        (kv,) = sum_blocks(kv, copies=2)
        kv = lax.all_to_all(kv, ("group", "pr"), 0, 0)

    with jax.named_scope("query"):
        query = queries(states_all, query_weight, batch)

    with jax.named_scope("attend"):
        branch = attend(tile_source, tile_count, row_request, query, kv, out_weight)

    with jax.named_scope("mix"):
        branch = [branch[0]] + [shift(branch[by], groups, FIRST, by) for by in HOPS[1:]]
        branch = sum_blocks(branch)
        branch = [branch[0]] + [shift(branch[by], groups, SECOND, by) for by in HOPS[1:]]
        return mix(attn_gate, states, branch)


def solution(mesh):
    groups = mesh.shape["group"]
    split = Mesh(mesh.devices.reshape(groups, SIDE, 2, 2), ("group",) + TP)
    in_specs = (
        P("group", None, None, TP),
        P(),
        P(),
        P("group", None),
        P(None, TP),
        P(TP),
        P(None, TP, None),
        P(None, TP),
        P(TP, None),
        P(TP),
        P(),
        P(None, "group", TP),
    )
    out_specs = P(None, "group", TP)
    return jax.shard_map(body, mesh=split, in_specs=in_specs, out_specs=out_specs, check_vma=False)
```

```python
import functools

import jax
import jax.numpy as jnp
from jax import lax
from jax.experimental import pallas as pl
from jax.experimental.pallas import tpu as pltpu
from jax.sharding import Mesh, PartitionSpec as P

D = 8192
KV_HEADS = 8
HEAD_DIM = 128
MAXT = 4
STEPS = 2
SIDE = 4
F32 = jnp.float32
BF16 = jnp.bfloat16
TP = ("z", "xh", "pr")
EVERY = ("group",) + TP
FIRST, SECOND = 0, 1
HOPS = (0, 1, 3, 2)
GRANT = 16 * 1024 * 1024
ANY = pl.BlockSpec(memory_space=pl.ANY)
IN_HBM = pl.BlockSpec(memory_space=pltpu.HBM)
IN_VMEM = pl.BlockSpec(memory_space=pltpu.VMEM)
IN_SMEM = pl.BlockSpec(memory_space=pltpu.SMEM)


def shift(value, groups, order, by):
    pairs = []
    for group in range(groups):
        for z in range(SIDE):
            for x in range(SIDE):
                if group % 2 == order:
                    other = z * SIDE + (x + by) % SIDE
                else:
                    other = (z + by) % SIDE * SIDE + x
                base = group * SIDE * SIDE
                pairs.append((base + z * SIDE + x, base + other))
    return lax.ppermute(value, EVERY, pairs)


def in_hbm(value):
    return pltpu.with_memory_space_constraint(value, pltpu.HBM)


def in_vmem(value):
    return pltpu.with_memory_space_constraint(value, pltpu.VMEM)


def kernel_call(kernel, operands, specs, out, scratch=(), flops=0, moved=0, transcendentals=0):
    return pl.pallas_call(
        kernel,
        in_specs=specs,
        out_specs=jax.tree.map(lambda _: IN_VMEM, out),
        out_shape=out,
        scratch_shapes=list(scratch),
        compiler_params=pltpu.CompilerParams(vmem_limit_bytes=GRANT),
        cost_estimate=pl.CostEstimate(
            flops=flops, bytes_accessed=moved, transcendentals=transcendentals
        ),
    )(*operands)


def wrap(value):
    return lax.rem(value + SIDE, SIDE)


def position():
    z = lax.axis_index("z")
    x = lax.axis_index("xh") * 2 + lax.axis_index("pr")
    return z, x, lax.rem(lax.axis_index("group"), 2)


def rank_from_here(first_by, second_by):
    z, x, core = position()
    first = jnp.where(core == 0, x, z)
    second = jnp.where(core == 0, z, x)
    first, second = wrap(first + first_by), wrap(second + second_by)
    return jnp.where(core == 0, second * SIDE + first, first * SIDE + second)


def join_kernel(moves, *refs):
    copies = []
    sem = refs[-1]
    for at, (source, low, target, first, count) in enumerate(moves):
        copies.append(
            pltpu.make_async_copy(
                refs[source].at[pl.ds(low, count)], refs[target].at[pl.ds(first, count)], sem.at[at]
            )
        )
    for copy in copies:
        copy.start()
    for copy in copies:
        copy.wait()


def join(arrays, moves, shapes, after=()):
    offset = len(arrays) + len(after)
    moves = [(a, low, offset + b, first, count) for a, low, b, first, count in moves]
    moved = 4 * sum(a.size for a in arrays)
    return kernel_call(
        functools.partial(join_kernel, moves),
        [*arrays, *after],
        [ANY] * offset,
        [pltpu.VMEM(shape, BF16) for shape in shapes],
        [pltpu.SemaphoreType.DMA((len(moves),))],
        moved=moved,
    )


def load_kernel(count, *refs):
    outs, sems = refs[-2 * count : -count], refs[-count:]
    copies = [pltpu.make_async_copy(refs[i], outs[i], sems[i]) for i in range(count)]
    for copy in copies:
        copy.start()
    for copy in copies:
        copy.wait()


def load(*values, after=()):
    return kernel_call(
        functools.partial(load_kernel, len(values)),
        [*map(in_hbm, values), *after],
        [IN_HBM] * len(values) + [ANY] * len(after),
        [pltpu.VMEM(value.shape, value.dtype) for value in values],
        [pltpu.SemaphoreType.DMA(()) for _ in values],
        moved=4 * sum(value.size for value in values),
    )


def fetcher(weight_ref, buffer, sem, shifts):
    z, x, core = position()
    first = jnp.where(core == 0, x, z)

    def fetch(by, start):
        at = shifts.index(by)
        to_x = pltpu.make_async_copy(
            weight_ref.at[:, wrap(first + by)], buffer.at[at], sem.at[at]
        )
        to_z = pltpu.make_async_copy(weight_ref.at[wrap(first + by)], buffer.at[at], sem.at[at])
        if start:
            pl.when(core == 0)(to_x.start)
            pl.when(core != 0)(to_z.start)
        else:
            to_z.wait()

    return fetch, jnp.where(core == 0, z, x)


def head_copies(kv_weight_ref, kv_buffer, kv_sem):
    span = pl.ds(pl.multiple_of(lax.axis_index("group") * HEAD_DIM, HEAD_DIM), HEAD_DIM)
    return [
        pltpu.make_async_copy(kv_weight_ref.at[i, :, span], kv_buffer.at[i], kv_sem.at[i])
        for i in range(2)
    ]


def contract_far_kernel(weight_ref, kv_weight_ref, states_ref, gain_ref, vision_ref, *refs):
    low_ref, high_ref, carried_ref, sent_ref = refs[:4]
    buffer, sem, kv_buffer, kv_sem, sent_sem = refs[4:]
    features = low_ref.shape[1]
    fetch, second = fetcher(weight_ref, buffer, sem, (2,))
    kv_copies = head_copies(kv_weight_ref, kv_buffer, kv_sem)
    for copy in kv_copies:
        copy.start()
    fetch(2, True)
    vision_copy = pltpu.make_async_copy(vision_ref, sent_ref, sent_sem)
    vision_copy.start()
    steps, batch, width = states_ref.shape
    carried_ref[: steps * batch] = states_ref[...].reshape(steps * batch, width)
    carried_ref[steps * batch :] = jnp.broadcast_to(gain_ref[...].reshape(1, -1), (16, width))
    for copy in kv_copies:
        copy.wait()
    weight = jnp.concatenate([kv_buffer[0], kv_buffer[1]], axis=1)
    fetch(2, False)
    for by in range(SIDE):
        rows = buffer[0, wrap(second + by)]
        part = jnp.dot(rows, weight, preferred_element_type=F32).astype(BF16)
        (low_ref if by < 2 else high_ref)[by % 2] = part
    vision_copy.wait()


def contract_near_kernel(weight_ref, kv_weight_ref, bias_ref, _, *refs):
    outs, biased_ref, (buffer, sem, kv_buffer, kv_sem) = refs[:3], refs[3], refs[4:]
    shifts = (1, 3, 0)
    features = outs[0].shape[1]
    fetch, second = fetcher(weight_ref, buffer, sem, shifts)
    kv_copies = head_copies(kv_weight_ref, kv_buffer, kv_sem)
    for copy in kv_copies:
        copy.start()
    for by in shifts:
        fetch(by, True)
    for copy in kv_copies:
        copy.wait()
    weight = jnp.concatenate([kv_buffer[0], kv_buffer[1]], axis=1)
    bias = jnp.broadcast_to(bias_ref[...].reshape(1, -1), (16, weight.shape[0]))
    biased_ref[...] = jnp.dot(bias, weight, preferred_element_type=F32)
    for out, by in zip(outs, shifts):
        fetch(by, False)
        rows = buffer[shifts.index(by)].reshape(SIDE * features, -1)
        part = jnp.dot(rows, weight, preferred_element_type=F32).astype(BF16)
        for at in range(SIDE):
            out[wrap(at - second)] = part[at * features : (at + 1) * features]


def contract_scratch(count, features, width):
    return [
        pltpu.VMEM((count, SIDE, features, width), BF16),
        pltpu.SemaphoreType.DMA((count,)),
        pltpu.VMEM((2, width, HEAD_DIM), BF16),
        pltpu.SemaphoreType.DMA((2,)),
    ]


def contract(proj_weight, kv_weight, proj_bias, states, norm_gain, vision_rows):
    total, width = proj_weight.shape
    features = vision_rows.shape[3]
    weight = in_hbm(proj_weight.reshape(SIDE, SIDE, features, width))
    kv_weight = in_hbm(kv_weight)
    flops = total * width * HEAD_DIM
    rows = states.shape[0] * states.shape[1] + 16
    low, high, carried, sent = kernel_call(
        contract_far_kernel,
        [weight, kv_weight, states, norm_gain, in_hbm(vision_rows)],
        [IN_HBM, IN_HBM, IN_VMEM, IN_VMEM, IN_HBM],
        [pltpu.VMEM((2, features, 2 * HEAD_DIM), BF16)] * 2
        + [
            jax.ShapeDtypeStruct((rows, states.shape[2]), BF16),
            pltpu.VMEM(vision_rows.shape, BF16),
        ],
        contract_scratch(1, features, width) + [pltpu.SemaphoreType.DMA(())],
        flops=flops,
        moved=4 * 1024 * 1024,
    )
    one, three, own, biased = kernel_call(
        contract_near_kernel,
        [weight, kv_weight, proj_bias, low],
        [IN_HBM, IN_HBM, IN_VMEM, ANY],
        [pltpu.VMEM((SIDE, features, 2 * HEAD_DIM), BF16)] * 3
        + [jax.ShapeDtypeStruct((16, 2 * HEAD_DIM), F32)],
        contract_scratch(3, features, width),
        flops=3 * flops,
        moved=10 * 1024 * 1024,
    )
    return low, high, one, three, own, biased, carried, sent


def merge_kernel(one_ref, low_ref, three_ref, high_ref, up_ref, down_ref):
    half = low_ref.shape[0]
    for at in range(2 * half):
        if at < half:
            up_ref[at] = (one_ref[at].astype(F32) + low_ref[at].astype(F32)).astype(BF16)
            down_ref[at] = three_ref[at]
        else:
            up_ref[at] = one_ref[at]
            down_ref[at] = (three_ref[at].astype(F32) + high_ref[at - half].astype(F32)).astype(
                BF16
            )


def merge(one, low, three, high):
    return kernel_call(
        merge_kernel,
        [in_vmem(value) for value in (one, low, three, high)],
        [IN_VMEM] * 4,
        [pltpu.VMEM(one.shape, BF16)] * 2,
        flops=one.size,
        moved=8 * one.size,
    )


def kv_kernel(same_ref, other_ref, merged_ref, biased_ref, *outs):
    bias = biased_ref[:1]
    for first_by in range(SIDE):
        for second_by in range(SIDE):
            rank = rank_from_here(first_by, second_by)
            tiles = [ref[at, rank] for ref in (same_ref, other_ref) for at in range(SIDE)]
            rows = jnp.concatenate(tiles, axis=0)
            part = jnp.dot(rows, merged_ref[...], preferred_element_type=F32)
            outs[first_by][second_by] = (part + bias).astype(BF16)


def kv_partials(same, other, merged, biased):
    _, tiles, tile_rows, features = same.shape
    count = 2 * SIDE * tile_rows
    return kernel_call(
        kv_kernel,
        [in_vmem(value) for value in (same, other, merged, biased)],
        [IN_VMEM] * 4,
        [pltpu.VMEM((SIDE, count, 2 * HEAD_DIM), BF16) for _ in range(SIDE)],
        flops=4 * count * tiles * features * HEAD_DIM,
        moved=12 * 1024 * 1024,
    )


def sum_kernel(*refs, sources, count):
    sources, outs = refs[:sources], refs[-count:]
    for at in range(count):
        total = sources[0][at].astype(F32)
        for source in sources[1:]:
            total = total + source[at].astype(F32)
        outs[at][...] = total.astype(BF16)


def sum_blocks(sources, after=()):
    count, rows, width = sources[0].shape
    return kernel_call(
        functools.partial(sum_kernel, sources=len(sources), count=count),
        [*map(in_vmem, sources), *after],
        [IN_VMEM] * len(sources) + [ANY] * len(after),
        [pltpu.VMEM((rows, width), BF16) for _ in range(count)],
        flops=len(sources) * sources[0].size,
        moved=10 * sources[0].size,
    )


def query_kernel(full_ref, weight_ref, out_ref, held, held_sem, buffer, sem):
    ranks, _, width = full_ref.shape
    batch = out_ref.shape[0]
    pieces = sem.shape[0]
    deep = buffer.shape[0] // pieces
    states = pltpu.make_async_copy(full_ref, held, held_sem)
    states.start()
    copies = [
        pltpu.make_async_copy(
            weight_ref.at[pl.ds(i * deep, deep)], buffer.at[pl.ds(i * deep, deep)], sem.at[i]
        )
        for i in range(pieces)
    ]
    for copy in copies:
        copy.start()
    states.wait()
    total = jnp.zeros((batch, 1), F32)
    for rank in range(ranks):
        hidden = held[rank, :batch, :].astype(F32)
        total += jnp.sum(hidden * hidden, axis=1, keepdims=True)
    inverse = lax.rsqrt(total / D + 1e-05)
    accum = jnp.zeros(out_ref.shape, F32)
    for rank in range(ranks):
        hidden = held[rank, :batch, :].astype(F32)
        gain = held[rank, batch : batch + 16, :].astype(F32)[:1]
        normed = (hidden * inverse * gain).astype(BF16)
        if rank * width % deep == 0:
            copies[rank * width // deep].wait()
        span = slice(rank * width, (rank + 1) * width)
        accum += jnp.dot(normed, buffer[span, :], preferred_element_type=F32)
    out_ref[...] = accum.astype(BF16)


def queries(full, query_weight, batch):
    columns = query_weight.shape[1]
    return kernel_call(
        query_kernel,
        [full, in_hbm(query_weight)],
        [ANY, IN_HBM],
        pltpu.VMEM((batch, columns), BF16),
        [
            pltpu.VMEM(full.shape, BF16),
            pltpu.SemaphoreType.DMA(()),
            pltpu.VMEM(query_weight.shape, BF16),
            pltpu.SemaphoreType.DMA((2,)),
        ],
        flops=2 * batch * D * columns,
        moved=12 * 1024 * 1024,
    )


def attend_kernel(
    source_ref, count_ref, request_ref, query_ref, own_ref, other_ref, weight_ref, *outs
):
    batch, width = query_ref.shape
    columns = outs[0].shape[2]
    half_rows = own_ref.shape[0]
    rows = 2 * half_rows
    slots = source_ref.shape[1]
    group = lax.axis_index("group")
    pair = lax.axis_index("pr")

    head = lax.axis_index("z") * 2 + lax.axis_index("xh")
    column = lax.broadcasted_iota(jnp.int32, (1, rows), 1) // (rows // slots)
    tile = jnp.zeros((1, rows), jnp.int32)
    for spot in range(slots):
        parity, far = spot // (slots // 2), spot % (slots // 2)
        encoder = wrap(head // 2 - HOPS[far % SIDE]) * 2 + lax.rem(head + far // SIDE, 2)
        tile = jnp.where(column == spot, encoder * 2 + lax.rem(parity + pair, 2), tile)
    owner = jnp.full((1, rows), -1, jnp.int32)
    for place in range(slots):
        request = place // MAXT
        valid = place % MAXT < count_ref[group * (slots // MAXT) + request]
        label = jnp.where(valid, request, -1)
        owner = jnp.where(tile == source_ref[group, place], label, owner)
    per_step = request_ref.shape[1]
    here = lax.broadcasted_iota(jnp.int32, (per_step, per_step), 0)
    there = lax.broadcasted_iota(jnp.int32, (per_step, per_step), 1)
    asked = jnp.where(here == there, request_ref[...], 0)
    asked = jnp.sum(asked, axis=1, keepdims=True)
    allowed = jnp.concatenate([asked] * (batch // per_step), axis=0) == owner

    keys = jnp.concatenate([own_ref[:, :HEAD_DIM], other_ref[:, :HEAD_DIM]], axis=0)
    values = jnp.concatenate([own_ref[:, HEAD_DIM:], other_ref[:, HEAD_DIM:]], axis=0)
    contexts = []
    for head in range(width // HEAD_DIM):
        span = slice(head * HEAD_DIM, (head + 1) * HEAD_DIM)
        scores = lax.dot_general(
            query_ref[:, span], keys, (((1,), (1,)), ((), ())), preferred_element_type=F32
        ) * (1.0 / HEAD_DIM**0.5)
        scores = jnp.where(allowed, scores, -1e30)
        largest = jnp.max(scores, axis=1, keepdims=True)
        weights = jnp.where(allowed, jnp.exp(scores - largest), 0.0)
        total = jnp.sum(weights, axis=1, keepdims=True)
        summed = jnp.dot(weights.astype(BF16), values, preferred_element_type=F32)
        contexts.append((summed / total).astype(BF16))
    context = jnp.concatenate(contexts, axis=1)
    for first_by in range(SIDE):
        for second_by in range(SIDE):
            rank = rank_from_here(first_by, second_by)
            span = pl.ds(pl.multiple_of(rank * columns, columns), columns)
            branch = jnp.dot(context, weight_ref[:, span], preferred_element_type=F32)
            outs[first_by][second_by] = branch.astype(BF16)


def attend(tile_source, tile_count, row_request, query, own, other, out_weight):
    batch, width = query.shape
    ranks = SIDE * SIDE
    columns = out_weight.shape[1] // ranks
    return kernel_call(
        attend_kernel,
        [tile_source, tile_count, row_request]
        + [in_vmem(value) for value in (query, own, other, out_weight)],
        [IN_SMEM, IN_SMEM] + [IN_VMEM] * 5,
        [pltpu.VMEM((SIDE, batch, columns), BF16) for _ in range(SIDE)],
        flops=2 * batch * width * out_weight.shape[1],
        moved=12 * 1024 * 1024,
        transcendentals=batch * 4 * 512,
    )


def mix_kernel(gate_ref, local_ref, *refs):
    sources, out_ref = refs[:SIDE], refs[SIDE]
    steps, batch, width = local_ref.shape
    gate = jnp.tanh(jnp.full((1, width), gate_ref[0, 0], F32))
    for step in range(steps):
        span = slice(step * batch, (step + 1) * batch)
        total = sources[0][span].astype(F32)
        for source in sources[1:]:
            total = total + source[span].astype(F32)
        out_ref[step] = (local_ref[step].astype(F32) + gate * total).astype(BF16)


def mix(gate, local, sources):
    return kernel_call(
        mix_kernel,
        [gate.reshape(1, 1), local, *map(in_vmem, sources)],
        [IN_SMEM, IN_VMEM] + [IN_VMEM] * SIDE,
        jax.ShapeDtypeStruct(local.shape, BF16),
        flops=SIDE * local.size,
        moved=12 * local.size,
    )


def body(
    vision_rows,
    tile_count,
    tile_source,
    row_request,
    proj_weight,
    proj_bias,
    kv_weight,
    query_weight,
    out_weight,
    norm_gain,
    attn_gate,
    states,
):
    groups = lax.axis_size("group")
    ranks = lax.axis_size(TP)
    tile_rows, features = vision_rows.shape[2:]
    per_group = vision_rows.shape[1] // groups
    slots = groups * per_group
    batch = STEPS * states.shape[1]
    width = states.shape[2]

    def spread(blocks, order):
        return [blocks[0]] + [shift(blocks[by], groups, order, by) for by in HOPS[1:]]

    def around(block, by):
        return lax.ppermute(block, "group", [(g, (g + 2 * by) % groups) for g in range(groups)])

    with jax.named_scope("contract"):
        low, high, one, three, own, biased, carried, sent = contract(
            proj_weight, kv_weight, proj_bias, states, norm_gain, vision_rows
        )
        low, high = shift(low, groups, FIRST, 1), shift(high, groups, FIRST, 3)

    with jax.named_scope("gather_states"):
        full = lax.all_gather(carried, TP)

    with jax.named_scope("gather_rows"):
        after, before = around(sent, 1), around(sent, 3)
        near = [sent, after, before, around(after, 1)]

    with jax.named_scope("contract"):
        up, down = merge(one, low, three, high)
        up, down = shift(up, groups, FIRST, 1), shift(down, groups, FIRST, 3)
        merged = sum_blocks([own, up, down], after=[near[3]])

    with jax.named_scope("gather_rows"):
        (same,) = join(
            near,
            [(i, 0, 0, i, 1) for i in range(SIDE)],
            [(SIDE, *vision_rows.shape[1:])],
            [merged[1]],
        )
        other = lax.ppermute(same, "group", [(g, g ^ 1) for g in range(groups)])

    with jax.named_scope("contract"):
        merged = [part[None] for part in spread(merged, SECOND)]
        (merged,) = sum_blocks(merged, after=[other])

    with jax.named_scope("kv"):
        kv = kv_partials(same, other, merged, biased)
        kv = sum_blocks(spread(kv, FIRST))
        kv = [part[None] for part in spread(kv, SECOND)]
        (out_here,) = load(out_weight, after=[full])
        (kv,) = sum_blocks(kv, after=[out_here])
        halves = []
        for flip in range(2):
            pairs = [
                (g * ranks + t, t // 2 * ranks + 2 * g + (t + flip) % 2)
                for g in range(groups)
                for t in range(ranks)
            ]
            halves.append(lax.ppermute(kv, EVERY, pairs))

    with jax.named_scope("query"):
        query = queries(full, query_weight, batch)

    with jax.named_scope("attend"):
        branch = attend(tile_source, tile_count, row_request, query, *halves, out_here)

    with jax.named_scope("mix"):
        branch = sum_blocks(spread(branch, FIRST))
        return mix(attn_gate, states, spread(branch, SECOND))


def solution(mesh):
    groups = mesh.shape["group"]
    split = Mesh(mesh.devices.reshape(groups, SIDE, 2, 2), ("group",) + TP)
    in_specs = (
        P("group", None, None, TP),
        P(),
        P(),
        P("group", None),
        P(None, TP),
        P(TP),
        P(None, TP, None),
        P(None, TP),
        P(TP, None),
        P(TP),
        P(),
        P(None, "group", TP),
    )
    out_specs = P(None, "group", TP)
    return jax.shard_map(body, mesh=split, in_specs=in_specs, out_specs=out_specs, check_vma=False)
```

```python
import functools

import jax
import jax.numpy as jnp
from jax import lax
from jax.experimental import pallas as pl
from jax.experimental.pallas import tpu as pltpu
from jax.sharding import Mesh, PartitionSpec as P

D = 8192
KV_HEADS = 8
HEAD_DIM = 128
MAXT = 4
STEPS = 2
SIDE = 4
F32 = jnp.float32
BF16 = jnp.bfloat16
TP = ("z", "xh", "pr")
EVERY = ("group",) + TP
FIRST, SECOND = 0, 1
HOPS = (0, 1, 3, 2)
GRANT = 16 * 1024 * 1024
ANY = pl.BlockSpec(memory_space=pl.ANY)
IN_HBM = pl.BlockSpec(memory_space=pltpu.HBM)
IN_VMEM = pl.BlockSpec(memory_space=pltpu.VMEM)
IN_SMEM = pl.BlockSpec(memory_space=pltpu.SMEM)


def shift(value, groups, order, by):
    pairs = []
    for group in range(groups):
        for z in range(SIDE):
            for x in range(SIDE):
                if group % 2 == order:
                    other = z * SIDE + (x + by) % SIDE
                else:
                    other = (z + by) % SIDE * SIDE + x
                base = group * SIDE * SIDE
                pairs.append((base + z * SIDE + x, base + other))
    return lax.ppermute(value, EVERY, pairs)


def in_hbm(value):
    return pltpu.with_memory_space_constraint(value, pltpu.HBM)


def in_vmem(value):
    return pltpu.with_memory_space_constraint(value, pltpu.VMEM)


def kernel_call(kernel, operands, specs, out, scratch=(), flops=0, moved=0, transcendentals=0):
    return pl.pallas_call(
        kernel,
        in_specs=specs,
        out_specs=jax.tree.map(lambda _: IN_VMEM, out),
        out_shape=out,
        scratch_shapes=list(scratch),
        compiler_params=pltpu.CompilerParams(vmem_limit_bytes=GRANT),
        cost_estimate=pl.CostEstimate(
            flops=flops, bytes_accessed=moved, transcendentals=transcendentals
        ),
    )(*operands)


def wrap(value):
    return lax.rem(value + SIDE, SIDE)


def position():
    z = lax.axis_index("z")
    x = lax.axis_index("xh") * 2 + lax.axis_index("pr")
    return z, x, lax.rem(lax.axis_index("group"), 2)


def rank_from_here(first_by, second_by):
    z, x, core = position()
    first = jnp.where(core == 0, x, z)
    second = jnp.where(core == 0, z, x)
    first, second = wrap(first + first_by), wrap(second + second_by)
    return jnp.where(core == 0, second * SIDE + first, first * SIDE + second)


def join_kernel(moves, *refs):
    copies = []
    sem = refs[-1]
    for at, (source, low, target, first, count) in enumerate(moves):
        copies.append(
            pltpu.make_async_copy(
                refs[source].at[pl.ds(low, count)], refs[target].at[pl.ds(first, count)], sem.at[at]
            )
        )
    for copy in copies:
        copy.start()
    for copy in copies:
        copy.wait()


def join(arrays, moves, shapes, after=()):
    offset = len(arrays) + len(after)
    moves = [(a, low, offset + b, first, count) for a, low, b, first, count in moves]
    moved = 4 * sum(a.size for a in arrays)
    return kernel_call(
        functools.partial(join_kernel, moves),
        [*arrays, *after],
        [ANY] * offset,
        [pltpu.VMEM(shape, BF16) for shape in shapes],
        [pltpu.SemaphoreType.DMA((len(moves),))],
        moved=moved,
    )


def load_kernel(count, *refs):
    outs, sems = refs[-2 * count : -count], refs[-count:]
    copies = [pltpu.make_async_copy(refs[i], outs[i], sems[i]) for i in range(count)]
    for copy in copies:
        copy.start()
    for copy in copies:
        copy.wait()


def load(*values, after=()):
    return kernel_call(
        functools.partial(load_kernel, len(values)),
        [*map(in_hbm, values), *after],
        [IN_HBM] * len(values) + [ANY] * len(after),
        [pltpu.VMEM(value.shape, value.dtype) for value in values],
        [pltpu.SemaphoreType.DMA(()) for _ in values],
        moved=4 * sum(value.size for value in values),
    )


def fetcher(weight_ref, buffer, sem, shifts):
    z, x, core = position()
    first = jnp.where(core == 0, x, z)

    def fetch(by, start):
        at = shifts.index(by)
        to_x = pltpu.make_async_copy(
            weight_ref.at[:, wrap(first + by)], buffer.at[at], sem.at[at]
        )
        to_z = pltpu.make_async_copy(weight_ref.at[wrap(first + by)], buffer.at[at], sem.at[at])
        if start:
            pl.when(core == 0)(to_x.start)
            pl.when(core != 0)(to_z.start)
        else:
            to_z.wait()

    return fetch, jnp.where(core == 0, z, x)


def head_copies(kv_weight_ref, kv_buffer, kv_sem):
    span = pl.ds(pl.multiple_of(lax.axis_index("group") * HEAD_DIM, HEAD_DIM), HEAD_DIM)
    return [
        pltpu.make_async_copy(kv_weight_ref.at[i, :, span], kv_buffer.at[i], kv_sem.at[i])
        for i in range(2)
    ]


def contract_far_kernel(weight_ref, kv_weight_ref, states_ref, gain_ref, vision_ref, *refs):
    low_ref, high_ref, carried_ref, sent_ref = refs[:4]
    buffer, sem, kv_buffer, kv_sem, gain_buffer, sent_sem = refs[4:]
    features = low_ref.shape[1]
    fetch, second = fetcher(weight_ref, buffer, sem, (2,))
    kv_copies = head_copies(kv_weight_ref, kv_buffer, kv_sem)
    for copy in kv_copies:
        copy.start()
    fetch(2, True)
    steps, batch, width = states_ref.shape
    others = [
        pltpu.make_async_copy(vision_ref, sent_ref, sent_sem.at[0]),
        pltpu.make_async_copy(gain_ref, gain_buffer, sent_sem.at[1]),
    ] + [
        pltpu.make_async_copy(
            states_ref.at[i], carried_ref.at[pl.ds(i * batch, batch)], sent_sem.at[2 + i]
        )
        for i in range(steps)
    ]
    for copy in others:
        copy.start()
    for copy in kv_copies:
        copy.wait()
    weight = jnp.concatenate([kv_buffer[0], kv_buffer[1]], axis=1)
    fetch(2, False)
    for by in range(SIDE):
        rows = buffer[0, wrap(second + by)]
        part = jnp.dot(rows, weight, preferred_element_type=F32).astype(BF16)
        (low_ref if by < 2 else high_ref)[by % 2] = part
    for copy in others:
        copy.wait()
    carried_ref[steps * batch :] = jnp.broadcast_to(gain_buffer[...].reshape(1, -1), (16, width))


def contract_near_kernel(weight_ref, kv_weight_ref, bias_ref, _, *refs):
    outs, biased_ref, (buffer, sem, kv_buffer, kv_sem) = refs[:3], refs[3], refs[4:]
    shifts = (1, 3, 0)
    features = outs[0].shape[1]
    fetch, second = fetcher(weight_ref, buffer, sem, shifts)
    kv_copies = head_copies(kv_weight_ref, kv_buffer, kv_sem)
    for copy in kv_copies:
        copy.start()
    for by in shifts:
        fetch(by, True)
    for copy in kv_copies:
        copy.wait()
    weight = jnp.concatenate([kv_buffer[0], kv_buffer[1]], axis=1)
    bias = jnp.broadcast_to(bias_ref[...].reshape(1, -1), (16, weight.shape[0]))
    biased_ref[...] = jnp.dot(bias, weight, preferred_element_type=F32)
    for out, by in zip(outs, shifts):
        fetch(by, False)
        rows = buffer[shifts.index(by)].reshape(SIDE * features, -1)
        part = jnp.dot(rows, weight, preferred_element_type=F32).astype(BF16)
        for at in range(SIDE):
            out[wrap(at - second)] = part[at * features : (at + 1) * features]


def contract_scratch(count, features, width):
    return [
        pltpu.VMEM((count, SIDE, features, width), BF16),
        pltpu.SemaphoreType.DMA((count,)),
        pltpu.VMEM((2, width, HEAD_DIM), BF16),
        pltpu.SemaphoreType.DMA((2,)),
    ]


def contract(proj_weight, kv_weight, proj_bias, states, norm_gain, vision_rows):
    total, width = proj_weight.shape
    features = vision_rows.shape[3]
    weight = in_hbm(proj_weight.reshape(SIDE, SIDE, features, width))
    kv_weight = in_hbm(kv_weight)
    flops = total * width * HEAD_DIM
    rows = states.shape[0] * states.shape[1] + 16
    low, high, carried, sent = kernel_call(
        contract_far_kernel,
        [weight, kv_weight, in_hbm(states), in_hbm(norm_gain), in_hbm(vision_rows)],
        [IN_HBM] * 5,
        [pltpu.VMEM((2, features, 2 * HEAD_DIM), BF16)] * 2
        + [
            jax.ShapeDtypeStruct((rows, states.shape[2]), BF16),
            pltpu.VMEM(vision_rows.shape, BF16),
        ],
        contract_scratch(1, features, width)
        + [pltpu.VMEM(norm_gain.shape, BF16), pltpu.SemaphoreType.DMA((2 + STEPS,))],
        flops=flops,
        moved=4 * 1024 * 1024,
    )
    one, three, own, biased = kernel_call(
        contract_near_kernel,
        [weight, kv_weight, proj_bias, low],
        [IN_HBM, IN_HBM, IN_VMEM, ANY],
        [pltpu.VMEM((SIDE, features, 2 * HEAD_DIM), BF16)] * 3
        + [jax.ShapeDtypeStruct((16, 2 * HEAD_DIM), F32)],
        contract_scratch(3, features, width),
        flops=3 * flops,
        moved=10 * 1024 * 1024,
    )
    return low, high, one, three, own, biased, carried, sent


def merge_kernel(one_ref, low_ref, three_ref, high_ref, up_ref, down_ref):
    half = low_ref.shape[0]
    for at in range(2 * half):
        if at < half:
            up_ref[at] = (one_ref[at].astype(F32) + low_ref[at].astype(F32)).astype(BF16)
            down_ref[at] = three_ref[at]
        else:
            up_ref[at] = one_ref[at]
            down_ref[at] = (three_ref[at].astype(F32) + high_ref[at - half].astype(F32)).astype(
                BF16
            )


def merge(one, low, three, high):
    return kernel_call(
        merge_kernel,
        [in_vmem(value) for value in (one, low, three, high)],
        [IN_VMEM] * 4,
        [pltpu.VMEM(one.shape, BF16)] * 2,
        flops=one.size,
        moved=8 * one.size,
    )


def kv_kernel(shifts, tokens, same_ref, other_ref, merged_ref, biased_ref, *refs):
    outs = refs[tokens:]
    bias = biased_ref[:1]
    for at, by in enumerate(shifts):
        for second_by in range(SIDE):
            rank = rank_from_here(by, second_by)
            tile = wrap(rank // SIDE - lax.axis_index("group") // 2) * SIDE + lax.rem(rank, SIDE)
            tiles = [ref[hop, tile] for ref in (same_ref, other_ref) for hop in range(SIDE)]
            rows = jnp.concatenate(tiles, axis=0)
            part = jnp.dot(rows, merged_ref[...], preferred_element_type=F32)
            part = (part + bias).astype(BF16)
            if len(shifts) == 1:
                outs[second_by // 2][second_by % 2] = part
            else:
                outs[at][second_by] = part


def kv_partials(same, other, merged, biased):
    _, tiles, tile_rows, features = same.shape
    count = 2 * SIDE * tile_rows
    operands = [in_vmem(value) for value in (same, other, merged, biased)]

    def call(shifts, shapes, after):
        return kernel_call(
            functools.partial(kv_kernel, shifts, len(after)),
            [*operands, *after],
            [IN_VMEM] * 4 + [ANY] * len(after),
            [pltpu.VMEM((size, count, 2 * HEAD_DIM), BF16) for size in shapes],
            flops=len(shifts) * count * tiles * features * HEAD_DIM,
            moved=len(shifts) * 3 * 1024 * 1024,
        )

    low, high = call((2,), (2, 2), [])
    one, three, own = call((1, 3, 0), (SIDE,) * 3, [low])
    return low, high, one, three, own


def sum_kernel(*refs, sources, count):
    sources, outs = refs[:sources], refs[-count:]
    for at in range(count):
        total = sources[0][at].astype(F32)
        for source in sources[1:]:
            total = total + source[at].astype(F32)
        outs[at][...] = total.astype(BF16)


def sum_blocks(sources, after=()):
    count, rows, width = sources[0].shape
    return kernel_call(
        functools.partial(sum_kernel, sources=len(sources), count=count),
        [*map(in_vmem, sources), *after],
        [IN_VMEM] * len(sources) + [ANY] * len(after),
        [pltpu.VMEM((rows, width), BF16) for _ in range(count)],
        flops=len(sources) * sources[0].size,
        moved=10 * sources[0].size,
    )


def query_kernel(batch, *refs):
    parts, (weight_ref, out_ref) = refs[:SIDE], refs[SIDE:]
    total = jnp.zeros((batch, 1), F32)
    for part in parts:
        for at in range(SIDE):
            hidden = part[at, :batch, :].astype(F32)
            total += jnp.sum(hidden * hidden, axis=1, keepdims=True)
    inverse = lax.rsqrt(total / D + 1e-05)
    accum = jnp.zeros(out_ref.shape, F32)
    for part, far in zip(parts, HOPS):
        width = part.shape[2]
        for at, near in enumerate(HOPS):
            hidden = part[at, :batch, :].astype(F32)
            gain = part[at, batch : batch + 16, :].astype(F32)[:1]
            normed = (hidden * inverse * gain).astype(BF16)
            rank = rank_from_here(-near, -far)
            rows = pl.ds(pl.multiple_of(rank * width, width), width)
            accum += jnp.dot(normed, weight_ref[rows, :], preferred_element_type=F32)
    out_ref[...] = accum.astype(BF16)


def queries(parts, query_weight, batch):
    columns = query_weight.shape[1]
    return kernel_call(
        functools.partial(query_kernel, batch),
        [*map(in_vmem, parts), in_vmem(query_weight)],
        [IN_VMEM] * (SIDE + 1),
        pltpu.VMEM((batch, columns), BF16),
        flops=2 * batch * D * columns,
        moved=12 * 1024 * 1024,
    )


def attend_kernel(
    source_ref, count_ref, request_ref, query_ref, own_ref, other_ref, weight_ref, *refs
):
    outs, context_ref = refs[:2], refs[2]
    batch, width = query_ref.shape
    half_rows = own_ref.shape[0]
    rows = 2 * half_rows
    slots = source_ref.shape[1]
    group = lax.axis_index("group")
    pair = lax.axis_index("pr")

    head = lax.axis_index("z") * 2 + lax.axis_index("xh")
    column = lax.broadcasted_iota(jnp.int32, (1, rows), 1) // (rows // slots)
    tile = jnp.zeros((1, rows), jnp.int32)
    for spot in range(slots):
        parity, far = spot // (slots // 2), spot % (slots // 2)
        encoder = wrap(head // 2 - HOPS[far % SIDE]) * 2 + lax.rem(head + far // SIDE, 2)
        tile = jnp.where(column == spot, encoder * 2 + lax.rem(parity + pair, 2), tile)
    owner = jnp.full((1, rows), -1, jnp.int32)
    for place in range(slots):
        request = place // MAXT
        valid = place % MAXT < count_ref[group * (slots // MAXT) + request]
        label = jnp.where(valid, request, -1)
        owner = jnp.where(tile == source_ref[group, place], label, owner)
    per_step = request_ref.shape[1]
    here = lax.broadcasted_iota(jnp.int32, (per_step, per_step), 0)
    there = lax.broadcasted_iota(jnp.int32, (per_step, per_step), 1)
    asked = jnp.where(here == there, request_ref[...], 0)
    asked = jnp.sum(asked, axis=1, keepdims=True)
    allowed = jnp.concatenate([asked] * (batch // per_step), axis=0) == owner

    keys = jnp.concatenate([own_ref[:, :HEAD_DIM], other_ref[:, :HEAD_DIM]], axis=0)
    values = jnp.concatenate([own_ref[:, HEAD_DIM:], other_ref[:, HEAD_DIM:]], axis=0)
    contexts = []
    for head in range(width // HEAD_DIM):
        span = slice(head * HEAD_DIM, (head + 1) * HEAD_DIM)
        scores = lax.dot_general(
            query_ref[:, span], keys, (((1,), (1,)), ((), ())), preferred_element_type=F32
        ) * (1.0 / HEAD_DIM**0.5)
        scores = jnp.where(allowed, scores, -1e30)
        largest = jnp.max(scores, axis=1, keepdims=True)
        weights = jnp.where(allowed, jnp.exp(scores - largest), 0.0)
        total = jnp.sum(weights, axis=1, keepdims=True)
        summed = jnp.dot(weights.astype(BF16), values, preferred_element_type=F32)
        contexts.append((summed / total).astype(BF16))
    context_ref[...] = jnp.concatenate(contexts, axis=1)
    branch_blocks(context_ref[...], weight_ref, (2,), outs)


def branch_blocks(context, weight_ref, shifts, outs):
    columns = outs[0].shape[2]
    for at, by in enumerate(shifts):
        for second_by in range(SIDE):
            rank = rank_from_here(by, second_by)
            span = pl.ds(pl.multiple_of(rank * columns, columns), columns)
            part = jnp.dot(context, weight_ref[:, span], preferred_element_type=F32).astype(BF16)
            if len(shifts) == 1:
                outs[second_by // 2][second_by % 2] = part
            else:
                outs[at][second_by] = part


def branch_kernel(context_ref, weight_ref, _, *outs):
    branch_blocks(context_ref[...], weight_ref, (1, 3, 0), outs)


def attend(tile_source, tile_count, row_request, query, own, other, out_weight):
    batch, width = query.shape
    columns = out_weight.shape[1] // (SIDE * SIDE)
    out_weight = in_vmem(out_weight)
    low, high, context = kernel_call(
        attend_kernel,
        [tile_source, tile_count, row_request, *map(in_vmem, (query, own, other)), out_weight],
        [IN_SMEM, IN_SMEM] + [IN_VMEM] * 5,
        [pltpu.VMEM((2, batch, columns), BF16)] * 2 + [pltpu.VMEM((batch, width), BF16)],
        flops=batch * width * out_weight.shape[1] // 2,
        moved=4 * 1024 * 1024,
        transcendentals=batch * 4 * 512,
    )
    one, three, own = kernel_call(
        branch_kernel,
        [in_vmem(context), out_weight, low],
        [IN_VMEM, IN_VMEM, ANY],
        [pltpu.VMEM((SIDE, batch, columns), BF16)] * 3,
        flops=3 * batch * width * out_weight.shape[1] // 2,
        moved=8 * 1024 * 1024,
    )
    return low, high, one, three, own


def mix_kernel(gate_ref, local_ref, *refs):
    sources, out_ref = refs[:SIDE], refs[SIDE]
    steps, batch, width = local_ref.shape
    gate = jnp.tanh(jnp.full((1, width), gate_ref[0, 0], F32))
    for step in range(steps):
        span = slice(step * batch, (step + 1) * batch)
        total = sources[0][span].astype(F32)
        for source in sources[1:]:
            total = total + source[span].astype(F32)
        out_ref[step] = (local_ref[step].astype(F32) + gate * total).astype(BF16)


def mix(gate, local, sources):
    return kernel_call(
        mix_kernel,
        [gate.reshape(1, 1), local, *map(in_vmem, sources)],
        [IN_SMEM, IN_VMEM] + [IN_VMEM] * SIDE,
        jax.ShapeDtypeStruct(local.shape, BF16),
        flops=SIDE * local.size,
        moved=12 * local.size,
    )


def body(
    vision_rows,
    tile_count,
    tile_source,
    row_request,
    proj_weight,
    proj_bias,
    kv_weight,
    query_weight,
    out_weight,
    norm_gain,
    attn_gate,
    states,
):
    groups = lax.axis_size("group")
    ranks = lax.axis_size(TP)
    tile_rows, features = vision_rows.shape[2:]
    per_group = vision_rows.shape[1] // groups
    slots = groups * per_group
    batch = STEPS * states.shape[1]
    width = states.shape[2]

    def spread(blocks, order):
        return [blocks[0]] + [shift(blocks[by], groups, order, by) for by in HOPS[1:]]

    def around(block, by):
        return lax.ppermute(block, "group", [(g, (g + 2 * by) % groups) for g in range(groups)])

    def first_sum(blocks, after=()):
        low, high, one, three, own = blocks
        low, high = shift(low, groups, FIRST, 1), shift(high, groups, FIRST, 3)
        up, down = merge(one, low, three, high)
        up, down = shift(up, groups, FIRST, 1), shift(down, groups, FIRST, 3)
        return sum_blocks([own, up, down], after)

    with jax.named_scope("contract"):
        *blocks, biased, carried, sent = contract(
            proj_weight, kv_weight, proj_bias, states, norm_gain, vision_rows
        )

    with jax.named_scope("load"):
        query_here, out_here = load(query_weight, out_weight, after=[carried])

    with jax.named_scope("gather_rows"):
        after, before = around(sent, 1), around(sent, 3)
        near = [sent, after, before, around(after, 1)]

    with jax.named_scope("contract"):
        merged = first_sum(blocks, [near[3], query_here, out_here])

    with jax.named_scope("gather_states"):
        (carried,) = join(
            [carried[None]], [(0, 0, 0, 0, 1)], [(1, *carried.shape)], [merged[1]]
        )
        arrived = [shift(carried, groups, FIRST, by) for by in HOPS[1:]]

    with jax.named_scope("gather_rows"):
        (same,) = join(
            near,
            [(i, 0, 0, i, 1) for i in range(SIDE)],
            [(SIDE, *vision_rows.shape[1:])],
            [merged[1]],
        )
        other = lax.ppermute(same, "group", [(g, g ^ 1) for g in range(groups)])

    with jax.named_scope("contract"):
        merged = [part[None] for part in spread(merged, SECOND)]
        (merged,) = sum_blocks(merged, after=[other, *arrived])

    with jax.named_scope("kv"):
        kv = kv_partials(same, other, merged, biased)

    with jax.named_scope("gather_states"):
        (states_near,) = join(
            [carried] + arrived,
            [(i, 0, 0, i, 1) for i in range(SIDE)],
            [(SIDE, *carried.shape[1:])],
            [kv[0]],
        )
        parts = spread([states_near] * SIDE, SECOND)

    with jax.named_scope("kv"):
        kv = first_sum(kv, parts[1:3])
        query = queries(parts, query_here, batch)
        kv = [part[None] for part in spread(kv, SECOND)]
        (kv,) = sum_blocks(kv)
        halves = []
        for flip in range(2):
            pairs = []
            for g in range(groups):
                for t in range(ranks):
                    tile = (t // SIDE - g // 2) % SIDE * SIDE + t % SIDE
                    home = tile // 2 * ranks + 2 * g + (tile + flip) % 2
                    pairs.append((g * ranks + t, home))
            halves.append(lax.ppermute(kv, EVERY, pairs))

    with jax.named_scope("attend"):
        branch = attend(tile_source, tile_count, row_request, query, *halves, out_here)

    with jax.named_scope("mix"):
        branch = first_sum(branch)
        return mix(attn_gate, states, spread(branch, SECOND))


def solution(mesh):
    groups = mesh.shape["group"]
    split = Mesh(mesh.devices.reshape(groups, SIDE, 2, 2), ("group",) + TP)
    in_specs = (
        P("group", None, None, TP),
        P(),
        P(),
        P("group", None),
        P(None, TP),
        P(TP),
        P(None, TP, None),
        P(None, TP),
        P(TP, None),
        P(TP),
        P(),
        P(None, "group", TP),
    )
    out_specs = P(None, "group", TP)
    return jax.shard_map(body, mesh=split, in_specs=in_specs, out_specs=out_specs, check_vma=False)
```

```python
import functools

import jax
import jax.numpy as jnp
from jax import lax
from jax.experimental import pallas as pl
from jax.experimental.pallas import tpu as pltpu
from jax.sharding import Mesh, PartitionSpec as P

D = 8192
KV_HEADS = 8
HEAD_DIM = 128
MAXT = 4
STEPS = 2
SIDE = 4
F32 = jnp.float32
BF16 = jnp.bfloat16
TP = ("z", "xh", "pr")
EVERY = ("group",) + TP
FIRST, SECOND = 0, 1
HOPS = (0, 1, 3, 2)
GRANT = 16 * 1024 * 1024
ANY = pl.BlockSpec(memory_space=pl.ANY)
IN_HBM = pl.BlockSpec(memory_space=pltpu.HBM)
IN_VMEM = pl.BlockSpec(memory_space=pltpu.VMEM)
IN_SMEM = pl.BlockSpec(memory_space=pltpu.SMEM)


def shift(value, groups, order, by):
    pairs = []
    for group in range(groups):
        for z in range(SIDE):
            for x in range(SIDE):
                if group % 2 == order:
                    other = z * SIDE + (x + by) % SIDE
                else:
                    other = (z + by) % SIDE * SIDE + x
                base = group * SIDE * SIDE
                pairs.append((base + z * SIDE + x, base + other))
    return lax.ppermute(value, EVERY, pairs)


def in_hbm(value):
    return pltpu.with_memory_space_constraint(value, pltpu.HBM)


def in_vmem(value):
    return pltpu.with_memory_space_constraint(value, pltpu.VMEM)


def kernel_call(kernel, operands, specs, out, scratch=(), flops=0, moved=0, transcendentals=0):
    return pl.pallas_call(
        kernel,
        in_specs=specs,
        out_specs=jax.tree.map(lambda _: IN_VMEM, out),
        out_shape=out,
        scratch_shapes=list(scratch),
        compiler_params=pltpu.CompilerParams(vmem_limit_bytes=GRANT),
        cost_estimate=pl.CostEstimate(
            flops=flops, bytes_accessed=moved, transcendentals=transcendentals
        ),
    )(*operands)


def wrap(value):
    return lax.rem(value + SIDE, SIDE)


def position():
    z = lax.axis_index("z")
    x = lax.axis_index("xh") * 2 + lax.axis_index("pr")
    return z, x, lax.rem(lax.axis_index("group"), 2)


def rank_from_here(first_by, second_by):
    z, x, core = position()
    first = jnp.where(core == 0, x, z)
    second = jnp.where(core == 0, z, x)
    first, second = wrap(first + first_by), wrap(second + second_by)
    return jnp.where(core == 0, second * SIDE + first, first * SIDE + second)


def join_kernel(moves, *refs):
    copies = []
    sem = refs[-1]
    for at, (source, low, target, first, count) in enumerate(moves):
        copies.append(
            pltpu.make_async_copy(
                refs[source].at[pl.ds(low, count)], refs[target].at[pl.ds(first, count)], sem.at[at]
            )
        )
    for copy in copies:
        copy.start()
    for copy in copies:
        copy.wait()


def join(arrays, moves, shapes, after=()):
    offset = len(arrays) + len(after)
    moves = [(a, low, offset + b, first, count) for a, low, b, first, count in moves]
    moved = 4 * sum(a.size for a in arrays)
    return kernel_call(
        functools.partial(join_kernel, moves),
        [*arrays, *after],
        [ANY] * offset,
        [pltpu.VMEM(shape, BF16) for shape in shapes],
        [pltpu.SemaphoreType.DMA((len(moves),))],
        moved=moved,
    )


def load_kernel(count, *refs):
    outs, sems = refs[-2 * count : -count], refs[-count:]
    copies = [pltpu.make_async_copy(refs[i], outs[i], sems[i]) for i in range(count)]
    for copy in copies:
        copy.start()
    for copy in copies:
        copy.wait()


def load(*values, after=()):
    return kernel_call(
        functools.partial(load_kernel, len(values)),
        [*map(in_hbm, values), *after],
        [IN_HBM] * len(values) + [ANY] * len(after),
        [pltpu.VMEM(value.shape, value.dtype) for value in values],
        [pltpu.SemaphoreType.DMA(()) for _ in values],
        moved=4 * sum(value.size for value in values),
    )


def fetcher(weight_ref, buffer, sem, shifts):
    z, x, core = position()
    first = jnp.where(core == 0, x, z)

    def fetch(by, start):
        at = shifts.index(by)
        to_x = pltpu.make_async_copy(
            weight_ref.at[:, wrap(first + by)], buffer.at[at], sem.at[at]
        )
        to_z = pltpu.make_async_copy(weight_ref.at[wrap(first + by)], buffer.at[at], sem.at[at])
        if start:
            pl.when(core == 0)(to_x.start)
            pl.when(core != 0)(to_z.start)
        else:
            to_z.wait()

    return fetch, jnp.where(core == 0, z, x)


def head_copies(kv_weight_ref, kv_buffer, kv_sem):
    span = pl.ds(pl.multiple_of(lax.axis_index("group") * HEAD_DIM, HEAD_DIM), HEAD_DIM)
    return [
        pltpu.make_async_copy(kv_weight_ref.at[i, :, span], kv_buffer.at[i], kv_sem.at[i])
        for i in range(2)
    ]


def contract_far_kernel(weight_ref, kv_weight_ref, states_ref, gain_ref, vision_ref, *refs):
    low_ref, high_ref, carried_ref, sent_ref = refs[:4]
    buffer, sem, kv_buffer, kv_sem, gain_buffer, sent_sem = refs[4:]
    features = low_ref.shape[1]
    fetch, second = fetcher(weight_ref, buffer, sem, (2,))
    kv_copies = head_copies(kv_weight_ref, kv_buffer, kv_sem)
    for copy in kv_copies:
        copy.start()
    fetch(2, True)
    steps, batch, width = states_ref.shape
    others = [
        pltpu.make_async_copy(vision_ref, sent_ref, sent_sem.at[0]),
        pltpu.make_async_copy(gain_ref, gain_buffer, sent_sem.at[1]),
    ] + [
        pltpu.make_async_copy(
            states_ref.at[i], carried_ref.at[pl.ds(i * batch, batch)], sent_sem.at[2 + i]
        )
        for i in range(steps)
    ]
    for copy in others:
        copy.start()
    for copy in kv_copies:
        copy.wait()
    weight = jnp.concatenate([kv_buffer[0], kv_buffer[1]], axis=1)
    fetch(2, False)
    for by in range(SIDE):
        rows = buffer[0, wrap(second + by)]
        part = jnp.dot(rows, weight, preferred_element_type=F32).astype(BF16)
        (low_ref if by < 2 else high_ref)[by % 2] = part
    for copy in others:
        copy.wait()
    carried_ref[steps * batch :] = jnp.broadcast_to(gain_buffer[...].reshape(1, -1), (16, width))


def contract_near_kernel(weight_ref, kv_weight_ref, bias_ref, _, *refs):
    outs, biased_ref, (buffer, sem, kv_buffer, kv_sem) = refs[:3], refs[3], refs[4:]
    shifts = (1, 3, 0)
    features = outs[0].shape[1]
    fetch, second = fetcher(weight_ref, buffer, sem, shifts)
    kv_copies = head_copies(kv_weight_ref, kv_buffer, kv_sem)
    for copy in kv_copies:
        copy.start()
    for by in shifts:
        fetch(by, True)
    for copy in kv_copies:
        copy.wait()
    weight = jnp.concatenate([kv_buffer[0], kv_buffer[1]], axis=1)
    bias = jnp.broadcast_to(bias_ref[...].reshape(1, -1), (16, weight.shape[0]))
    biased_ref[...] = jnp.dot(bias, weight, preferred_element_type=F32)
    for out, by in zip(outs, shifts):
        fetch(by, False)
        rows = buffer[shifts.index(by)].reshape(SIDE * features, -1)
        part = jnp.dot(rows, weight, preferred_element_type=F32).astype(BF16)
        for at in range(SIDE):
            out[wrap(at - second)] = part[at * features : (at + 1) * features]


def contract_scratch(count, features, width):
    return [
        pltpu.VMEM((count, SIDE, features, width), BF16),
        pltpu.SemaphoreType.DMA((count,)),
        pltpu.VMEM((2, width, HEAD_DIM), BF16),
        pltpu.SemaphoreType.DMA((2,)),
    ]


def contract(proj_weight, kv_weight, proj_bias, states, norm_gain, vision_rows):
    total, width = proj_weight.shape
    features = vision_rows.shape[3]
    weight = in_hbm(proj_weight.reshape(SIDE, SIDE, features, width))
    kv_weight = in_hbm(kv_weight)
    flops = total * width * HEAD_DIM
    rows = states.shape[0] * states.shape[1] + 16
    low, high, carried, sent = kernel_call(
        contract_far_kernel,
        [weight, kv_weight, in_hbm(states), in_hbm(norm_gain), in_hbm(vision_rows)],
        [IN_HBM] * 5,
        [pltpu.VMEM((2, features, 2 * HEAD_DIM), BF16)] * 2
        + [
            jax.ShapeDtypeStruct((rows, states.shape[2]), BF16),
            pltpu.VMEM(vision_rows.shape, BF16),
        ],
        contract_scratch(1, features, width)
        + [pltpu.VMEM(norm_gain.shape, BF16), pltpu.SemaphoreType.DMA((2 + STEPS,))],
        flops=flops,
        moved=4 * 1024 * 1024,
    )
    one, three, own, biased = kernel_call(
        contract_near_kernel,
        [weight, kv_weight, proj_bias, low],
        [IN_HBM, IN_HBM, IN_VMEM, ANY],
        [pltpu.VMEM((SIDE, features, 2 * HEAD_DIM), BF16)] * 3
        + [jax.ShapeDtypeStruct((16, 2 * HEAD_DIM), F32)],
        contract_scratch(3, features, width),
        flops=3 * flops,
        moved=10 * 1024 * 1024,
    )
    return low, high, one, three, own, biased, carried, sent


def merge_kernel(one_ref, low_ref, three_ref, high_ref, up_ref, down_ref):
    half = low_ref.shape[0]
    for at in range(2 * half):
        if at < half:
            up_ref[at] = (one_ref[at].astype(F32) + low_ref[at].astype(F32)).astype(BF16)
            down_ref[at] = three_ref[at]
        else:
            up_ref[at] = one_ref[at]
            down_ref[at] = (three_ref[at].astype(F32) + high_ref[at - half].astype(F32)).astype(
                BF16
            )


def merge(one, low, three, high):
    return kernel_call(
        merge_kernel,
        [in_vmem(value) for value in (one, low, three, high)],
        [IN_VMEM] * 4,
        [pltpu.VMEM(one.shape, BF16)] * 2,
        flops=one.size,
        moved=8 * one.size,
    )


def kv_kernel(shifts, tokens, same_ref, other_ref, merged_ref, biased_ref, *refs):
    outs = refs[tokens:]
    bias = biased_ref[:1]
    for at, by in enumerate(shifts):
        for second_by in range(SIDE):
            rank = rank_from_here(by, second_by)
            tile = wrap(rank // SIDE - lax.axis_index("group") // 2) * SIDE + lax.rem(rank, SIDE)
            tiles = [ref[hop, tile] for ref in (same_ref, other_ref) for hop in range(SIDE)]
            rows = jnp.concatenate(tiles, axis=0)
            part = jnp.dot(rows, merged_ref[...], preferred_element_type=F32)
            part = (part + bias).astype(BF16)
            if len(shifts) == 1:
                outs[second_by // 2][second_by % 2] = part
            else:
                outs[at][second_by] = part


def kv_partials(same, other, merged, biased):
    _, tiles, tile_rows, features = same.shape
    count = 2 * SIDE * tile_rows
    operands = [in_vmem(value) for value in (same, other, merged, biased)]

    def call(shifts, shapes, after):
        return kernel_call(
            functools.partial(kv_kernel, shifts, len(after)),
            [*operands, *after],
            [IN_VMEM] * 4 + [ANY] * len(after),
            [pltpu.VMEM((size, count, 2 * HEAD_DIM), BF16) for size in shapes],
            flops=len(shifts) * count * tiles * features * HEAD_DIM,
            moved=len(shifts) * 3 * 1024 * 1024,
        )

    low, high = call((2,), (2, 2), [])
    one, three, own = call((1, 3, 0), (SIDE,) * 3, [low])
    return low, high, one, three, own


def sum_kernel(*refs, sources, count):
    sources, outs = refs[:sources], refs[-count:]
    for at in range(count):
        total = sources[0][at].astype(F32)
        for source in sources[1:]:
            total = total + source[at].astype(F32)
        outs[at][...] = total.astype(BF16)


def sum_blocks(sources, after=()):
    count, rows, width = sources[0].shape
    return kernel_call(
        functools.partial(sum_kernel, sources=len(sources), count=count),
        [*map(in_vmem, sources), *after],
        [IN_VMEM] * len(sources) + [ANY] * len(after),
        [pltpu.VMEM((rows, width), BF16) for _ in range(count)],
        flops=len(sources) * sources[0].size,
        moved=10 * sources[0].size,
    )


def query_kernel(batch, *refs):
    parts, (weight_ref, out_ref) = refs[:SIDE], refs[SIDE:]
    total = jnp.zeros((batch, 1), F32)
    for part in parts:
        for at in range(SIDE):
            hidden = part[at, :batch, :].astype(F32)
            total += jnp.sum(hidden * hidden, axis=1, keepdims=True)
    inverse = lax.rsqrt(total / D + 1e-05)
    accum = jnp.zeros(out_ref.shape, F32)
    for part, far in zip(parts, HOPS):
        width = part.shape[2]
        for at, near in enumerate(HOPS):
            hidden = part[at, :batch, :].astype(F32)
            gain = part[at, batch : batch + 16, :].astype(F32)[:1]
            normed = (hidden * inverse * gain).astype(BF16)
            rank = rank_from_here(-near, -far)
            rows = pl.ds(pl.multiple_of(rank * width, width), width)
            accum += jnp.dot(normed, weight_ref[rows, :], preferred_element_type=F32)
    out_ref[...] = accum.astype(BF16)


def queries(parts, query_weight, batch):
    columns = query_weight.shape[1]
    return kernel_call(
        functools.partial(query_kernel, batch),
        [*map(in_vmem, parts), in_vmem(query_weight)],
        [IN_VMEM] * (SIDE + 1),
        pltpu.VMEM((batch, columns), BF16),
        flops=2 * batch * D * columns,
        moved=12 * 1024 * 1024,
    )


def attend_kernel(
    source_ref, count_ref, request_ref, query_ref, own_ref, other_ref, weight_ref, *outs
):
    batch, width = query_ref.shape
    half_rows = own_ref.shape[0]
    rows = 2 * half_rows
    slots = source_ref.shape[1]
    group = lax.axis_index("group")
    pair = lax.axis_index("pr")

    head = lax.axis_index("z") * 2 + lax.axis_index("xh")
    column = lax.broadcasted_iota(jnp.int32, (1, rows), 1) // (rows // slots)
    tile = jnp.zeros((1, rows), jnp.int32)
    for spot in range(slots):
        parity, far = spot // (slots // 2), spot % (slots // 2)
        encoder = wrap(head // 2 - HOPS[far % SIDE]) * 2 + lax.rem(head + far // SIDE, 2)
        tile = jnp.where(column == spot, encoder * 2 + lax.rem(parity + pair, 2), tile)
    owner = jnp.full((1, rows), -1, jnp.int32)
    for place in range(slots):
        request = place // MAXT
        valid = place % MAXT < count_ref[group * (slots // MAXT) + request]
        label = jnp.where(valid, request, -1)
        owner = jnp.where(tile == source_ref[group, place], label, owner)
    per_step = request_ref.shape[1]
    here = lax.broadcasted_iota(jnp.int32, (per_step, per_step), 0)
    there = lax.broadcasted_iota(jnp.int32, (per_step, per_step), 1)
    asked = jnp.where(here == there, request_ref[...], 0)
    asked = jnp.sum(asked, axis=1, keepdims=True)
    allowed = jnp.concatenate([asked] * (batch // per_step), axis=0) == owner

    keys = jnp.concatenate([own_ref[:, :HEAD_DIM], other_ref[:, :HEAD_DIM]], axis=0)
    values = jnp.concatenate([own_ref[:, HEAD_DIM:], other_ref[:, HEAD_DIM:]], axis=0)
    contexts = []
    for head in range(width // HEAD_DIM):
        span = slice(head * HEAD_DIM, (head + 1) * HEAD_DIM)
        scores = lax.dot_general(
            query_ref[:, span], keys, (((1,), (1,)), ((), ())), preferred_element_type=F32
        ) * (1.0 / HEAD_DIM**0.5)
        scores = jnp.where(allowed, scores, -1e30)
        largest = jnp.max(scores, axis=1, keepdims=True)
        weights = jnp.where(allowed, jnp.exp(scores - largest), 0.0)
        total = jnp.sum(weights, axis=1, keepdims=True)
        summed = jnp.dot(weights.astype(BF16), values, preferred_element_type=F32)
        contexts.append((summed / total).astype(BF16))
    context = jnp.concatenate(contexts, axis=1)
    columns = outs[0].shape[2]
    for first_by in range(SIDE):
        for second_by in range(SIDE):
            rank = rank_from_here(first_by, second_by)
            span = pl.ds(pl.multiple_of(rank * columns, columns), columns)
            branch = jnp.dot(context, weight_ref[:, span], preferred_element_type=F32)
            outs[first_by][second_by] = branch.astype(BF16)


def attend(tile_source, tile_count, row_request, query, own, other, out_weight):
    batch, width = query.shape
    columns = out_weight.shape[1] // (SIDE * SIDE)
    return kernel_call(
        attend_kernel,
        [tile_source, tile_count, row_request]
        + [in_vmem(value) for value in (query, own, other, out_weight)],
        [IN_SMEM, IN_SMEM] + [IN_VMEM] * 5,
        [pltpu.VMEM((SIDE, batch, columns), BF16) for _ in range(SIDE)],
        flops=2 * batch * width * out_weight.shape[1],
        moved=12 * 1024 * 1024,
        transcendentals=batch * 4 * 512,
    )


def mix_kernel(gate_ref, local_ref, *refs):
    sources, out_ref = refs[:SIDE], refs[SIDE]
    steps, batch, width = local_ref.shape
    gate = jnp.tanh(jnp.full((1, width), gate_ref[0, 0], F32))
    for step in range(steps):
        span = slice(step * batch, (step + 1) * batch)
        total = sources[0][span].astype(F32)
        for source in sources[1:]:
            total = total + source[span].astype(F32)
        out_ref[step] = (local_ref[step].astype(F32) + gate * total).astype(BF16)


def mix(gate, local, sources):
    return kernel_call(
        mix_kernel,
        [gate.reshape(1, 1), local, *map(in_vmem, sources)],
        [IN_SMEM, IN_VMEM] + [IN_VMEM] * SIDE,
        jax.ShapeDtypeStruct(local.shape, BF16),
        flops=SIDE * local.size,
        moved=12 * local.size,
    )


def body(
    vision_rows,
    tile_count,
    tile_source,
    row_request,
    proj_weight,
    proj_bias,
    kv_weight,
    query_weight,
    out_weight,
    norm_gain,
    attn_gate,
    states,
):
    groups = lax.axis_size("group")
    ranks = lax.axis_size(TP)
    tile_rows, features = vision_rows.shape[2:]
    per_group = vision_rows.shape[1] // groups
    slots = groups * per_group
    batch = STEPS * states.shape[1]
    width = states.shape[2]

    def spread(blocks, order):
        return [blocks[0]] + [shift(blocks[by], groups, order, by) for by in HOPS[1:]]

    def around(block, by):
        return lax.ppermute(block, "group", [(g, (g + 2 * by) % groups) for g in range(groups)])

    def first_sum(blocks, after=()):
        low, high, one, three, own = blocks
        low, high = shift(low, groups, FIRST, 1), shift(high, groups, FIRST, 3)
        up, down = merge(one, low, three, high)
        up, down = shift(up, groups, FIRST, 1), shift(down, groups, FIRST, 3)
        return sum_blocks([own, up, down], after)

    with jax.named_scope("contract"):
        *blocks, biased, carried, sent = contract(
            proj_weight, kv_weight, proj_bias, states, norm_gain, vision_rows
        )

    with jax.named_scope("load"):
        query_here, out_here = load(query_weight, out_weight, after=[carried])

    with jax.named_scope("gather_rows"):
        after, before = around(sent, 1), around(sent, 3)
        near = [sent, after, before, around(after, 1)]

    with jax.named_scope("contract"):
        merged = first_sum(blocks, [near[3], query_here, out_here])

    with jax.named_scope("gather_rows"):
        (same,) = join(
            near,
            [(i, 0, 0, i, 1) for i in range(SIDE)],
            [(SIDE, *vision_rows.shape[1:])],
            [merged[1]],
        )
        other = lax.ppermute(same, "group", [(g, g ^ 1) for g in range(groups)])

    with jax.named_scope("gather_states"):
        (carried,) = join(
            [carried[None]], [(0, 0, 0, 0, 1)], [(1, *carried.shape)], [other]
        )
        arrived = [shift(carried, groups, FIRST, by) for by in HOPS[1:]]

    with jax.named_scope("contract"):
        merged = [part[None] for part in spread(merged, SECOND)]
        (merged,) = sum_blocks(merged, after=[other, *arrived])

    with jax.named_scope("kv"):
        kv = kv_partials(same, other, merged, biased)

    with jax.named_scope("gather_states"):
        (states_near,) = join(
            [carried] + arrived,
            [(i, 0, 0, i, 1) for i in range(SIDE)],
            [(SIDE, *carried.shape[1:])],
            [kv[0]],
        )
        parts = spread([states_near] * SIDE, SECOND)

    with jax.named_scope("kv"):
        kv = first_sum(kv, parts[1:3])
        query = queries(parts, query_here, batch)
        kv = [part[None] for part in spread(kv, SECOND)]
        (kv,) = sum_blocks(kv)
        halves = []
        for flip in range(2):
            pairs = []
            for g in range(groups):
                for t in range(ranks):
                    tile = (t // SIDE - g // 2) % SIDE * SIDE + t % SIDE
                    home = tile // 2 * ranks + 2 * g + (tile + flip) % 2
                    pairs.append((g * ranks + t, home))
            halves.append(lax.ppermute(kv, EVERY, pairs))

    with jax.named_scope("attend"):
        branch = attend(tile_source, tile_count, row_request, query, *halves, out_here)

    with jax.named_scope("mix"):
        branch = sum_blocks(spread(branch, FIRST))
        return mix(attn_gate, states, spread(branch, SECOND))


def solution(mesh):
    groups = mesh.shape["group"]
    split = Mesh(mesh.devices.reshape(groups, SIDE, 2, 2), ("group",) + TP)
    in_specs = (
        P("group", None, None, TP),
        P(),
        P(),
        P("group", None),
        P(None, TP),
        P(TP),
        P(None, TP, None),
        P(None, TP),
        P(TP, None),
        P(TP),
        P(),
        P(None, "group", TP),
    )
    out_specs = P(None, "group", TP)
    return jax.shard_map(body, mesh=split, in_specs=in_specs, out_specs=out_specs, check_vma=False)
```

```python
import functools

import jax
import jax.numpy as jnp
from jax import lax
from jax.experimental import pallas as pl
from jax.experimental.pallas import tpu as pltpu
from jax.sharding import Mesh, PartitionSpec as P

D = 8192
KV_HEADS = 8
HEAD_DIM = 128
MAXT = 4
STEPS = 2
SIDE = 4
F32 = jnp.float32
BF16 = jnp.bfloat16
TP = ("z", "xh", "pr")
EVERY = ("group",) + TP
FIRST, SECOND = 0, 1
HOPS = (0, 1, 3, 2)
GRANT = 16 * 1024 * 1024
ANY = pl.BlockSpec(memory_space=pl.ANY)
IN_HBM = pl.BlockSpec(memory_space=pltpu.HBM)
IN_VMEM = pl.BlockSpec(memory_space=pltpu.VMEM)
IN_SMEM = pl.BlockSpec(memory_space=pltpu.SMEM)


def shift(value, groups, order, by):
    pairs = []
    for group in range(groups):
        for z in range(SIDE):
            for x in range(SIDE):
                if group % 2 == order:
                    other = z * SIDE + (x + by) % SIDE
                else:
                    other = (z + by) % SIDE * SIDE + x
                base = group * SIDE * SIDE
                pairs.append((base + z * SIDE + x, base + other))
    return lax.ppermute(value, EVERY, pairs)


def in_hbm(value):
    return pltpu.with_memory_space_constraint(value, pltpu.HBM)


def in_vmem(value):
    return pltpu.with_memory_space_constraint(value, pltpu.VMEM)


def kernel_call(kernel, operands, specs, out, scratch=(), flops=0, moved=0, transcendentals=0):
    return pl.pallas_call(
        kernel,
        in_specs=specs,
        out_specs=jax.tree.map(lambda _: IN_VMEM, out),
        out_shape=out,
        scratch_shapes=list(scratch),
        compiler_params=pltpu.CompilerParams(vmem_limit_bytes=GRANT),
        cost_estimate=pl.CostEstimate(
            flops=flops, bytes_accessed=moved, transcendentals=transcendentals
        ),
    )(*operands)


def wrap(value):
    return lax.rem(value + SIDE, SIDE)


def position():
    z = lax.axis_index("z")
    x = lax.axis_index("xh") * 2 + lax.axis_index("pr")
    return z, x, lax.rem(lax.axis_index("group"), 2)


def rank_from_here(first_by, second_by):
    z, x, core = position()
    first = jnp.where(core == 0, x, z)
    second = jnp.where(core == 0, z, x)
    first, second = wrap(first + first_by), wrap(second + second_by)
    return jnp.where(core == 0, second * SIDE + first, first * SIDE + second)


def join_kernel(moves, *refs):
    copies = []
    sem = refs[-1]
    for at, (source, low, target, first, count) in enumerate(moves):
        copies.append(
            pltpu.make_async_copy(
                refs[source].at[pl.ds(low, count)], refs[target].at[pl.ds(first, count)], sem.at[at]
            )
        )
    for copy in copies:
        copy.start()
    for copy in copies:
        copy.wait()


def join(arrays, moves, shapes, after=()):
    offset = len(arrays) + len(after)
    moves = [(a, low, offset + b, first, count) for a, low, b, first, count in moves]
    moved = 4 * sum(a.size for a in arrays)
    return kernel_call(
        functools.partial(join_kernel, moves),
        [*arrays, *after],
        [ANY] * offset,
        [pltpu.VMEM(shape, BF16) for shape in shapes],
        [pltpu.SemaphoreType.DMA((len(moves),))],
        moved=moved,
    )


def load_kernel(count, *refs):
    outs, sems = refs[-2 * count : -count], refs[-count:]
    copies = [pltpu.make_async_copy(refs[i], outs[i], sems[i]) for i in range(count)]
    for copy in copies:
        copy.start()
    for copy in copies:
        copy.wait()


def load(*values, after=()):
    return kernel_call(
        functools.partial(load_kernel, len(values)),
        [*map(in_hbm, values), *after],
        [IN_HBM] * len(values) + [ANY] * len(after),
        [pltpu.VMEM(value.shape, value.dtype) for value in values],
        [pltpu.SemaphoreType.DMA(()) for _ in values],
        moved=4 * sum(value.size for value in values),
    )


def fetcher(weight_ref, buffer, sem, shifts):
    z, x, core = position()
    first = jnp.where(core == 0, x, z)

    def fetch(by, start):
        at = shifts.index(by)
        to_x = pltpu.make_async_copy(
            weight_ref.at[:, wrap(first + by)], buffer.at[at], sem.at[at]
        )
        to_z = pltpu.make_async_copy(weight_ref.at[wrap(first + by)], buffer.at[at], sem.at[at])
        if start:
            pl.when(core == 0)(to_x.start)
            pl.when(core != 0)(to_z.start)
        else:
            to_z.wait()

    return fetch, jnp.where(core == 0, z, x)


def head_copies(kv_weight_ref, kv_buffer, kv_sem):
    span = pl.ds(pl.multiple_of(lax.axis_index("group") * HEAD_DIM, HEAD_DIM), HEAD_DIM)
    return [
        pltpu.make_async_copy(kv_weight_ref.at[i, :, span], kv_buffer.at[i], kv_sem.at[i])
        for i in range(2)
    ]


def contract_far_kernel(weight_ref, kv_weight_ref, states_ref, gain_ref, vision_ref, *refs):
    low_ref, high_ref, carried_ref, sent_ref = refs[:4]
    buffer, sem, kv_buffer, kv_sem, gain_buffer, sent_sem = refs[4:]
    features = low_ref.shape[1]
    fetch, second = fetcher(weight_ref, buffer, sem, (2,))
    kv_copies = head_copies(kv_weight_ref, kv_buffer, kv_sem)
    for copy in kv_copies:
        copy.start()
    fetch(2, True)
    steps, batch, width = states_ref.shape
    others = [
        pltpu.make_async_copy(vision_ref, sent_ref, sent_sem.at[0]),
        pltpu.make_async_copy(gain_ref, gain_buffer, sent_sem.at[1]),
    ] + [
        pltpu.make_async_copy(
            states_ref.at[i], carried_ref.at[pl.ds(i * batch, batch)], sent_sem.at[2 + i]
        )
        for i in range(steps)
    ]
    for copy in others:
        copy.start()
    for copy in kv_copies:
        copy.wait()
    weight = jnp.concatenate([kv_buffer[0], kv_buffer[1]], axis=1)
    fetch(2, False)
    for by in range(SIDE):
        rows = buffer[0, wrap(second + by)]
        part = jnp.dot(rows, weight, preferred_element_type=F32).astype(BF16)
        (low_ref if by < 2 else high_ref)[by % 2] = part
    for copy in others:
        copy.wait()
    carried_ref[steps * batch :] = jnp.broadcast_to(gain_buffer[...].reshape(1, -1), (16, width))


def contract_near_kernel(weight_ref, kv_weight_ref, bias_ref, _, *refs):
    outs, biased_ref, (buffer, sem, kv_buffer, kv_sem) = refs[:3], refs[3], refs[4:]
    shifts = (1, 3, 0)
    features = outs[0].shape[1]
    fetch, second = fetcher(weight_ref, buffer, sem, shifts)
    kv_copies = head_copies(kv_weight_ref, kv_buffer, kv_sem)
    for copy in kv_copies:
        copy.start()
    for by in shifts:
        fetch(by, True)
    for copy in kv_copies:
        copy.wait()
    weight = jnp.concatenate([kv_buffer[0], kv_buffer[1]], axis=1)
    bias = jnp.broadcast_to(bias_ref[...].reshape(1, -1), (16, weight.shape[0]))
    biased_ref[...] = jnp.dot(bias, weight, preferred_element_type=F32)
    for out, by in zip(outs, shifts):
        fetch(by, False)
        rows = buffer[shifts.index(by)].reshape(SIDE * features, -1)
        part = jnp.dot(rows, weight, preferred_element_type=F32).astype(BF16)
        for at in range(SIDE):
            out[wrap(at - second)] = part[at * features : (at + 1) * features]


def contract_scratch(count, features, width):
    return [
        pltpu.VMEM((count, SIDE, features, width), BF16),
        pltpu.SemaphoreType.DMA((count,)),
        pltpu.VMEM((2, width, HEAD_DIM), BF16),
        pltpu.SemaphoreType.DMA((2,)),
    ]


def contract(proj_weight, kv_weight, proj_bias, states, norm_gain, vision_rows):
    total, width = proj_weight.shape
    features = vision_rows.shape[3]
    weight = in_hbm(proj_weight.reshape(SIDE, SIDE, features, width))
    kv_weight = in_hbm(kv_weight)
    flops = total * width * HEAD_DIM
    rows = states.shape[0] * states.shape[1] + 16
    low, high, carried, sent = kernel_call(
        contract_far_kernel,
        [weight, kv_weight, in_hbm(states), in_hbm(norm_gain), in_hbm(vision_rows)],
        [IN_HBM] * 5,
        [pltpu.VMEM((2, features, 2 * HEAD_DIM), BF16)] * 2
        + [
            jax.ShapeDtypeStruct((rows, states.shape[2]), BF16),
            pltpu.VMEM(vision_rows.shape, BF16),
        ],
        contract_scratch(1, features, width)
        + [pltpu.VMEM(norm_gain.shape, BF16), pltpu.SemaphoreType.DMA((2 + STEPS,))],
        flops=flops,
        moved=4 * 1024 * 1024,
    )
    one, three, own, biased = kernel_call(
        contract_near_kernel,
        [weight, kv_weight, proj_bias, low],
        [IN_HBM, IN_HBM, IN_VMEM, ANY],
        [pltpu.VMEM((SIDE, features, 2 * HEAD_DIM), BF16)] * 3
        + [jax.ShapeDtypeStruct((16, 2 * HEAD_DIM), F32)],
        contract_scratch(3, features, width),
        flops=3 * flops,
        moved=10 * 1024 * 1024,
    )
    return low, high, one, three, own, biased, carried, sent


def merge_kernel(one_ref, low_ref, three_ref, high_ref, up_ref, down_ref):
    half = low_ref.shape[0]
    for at in range(2 * half):
        if at < half:
            up_ref[at] = (one_ref[at].astype(F32) + low_ref[at].astype(F32)).astype(BF16)
            down_ref[at] = three_ref[at]
        else:
            up_ref[at] = one_ref[at]
            down_ref[at] = (three_ref[at].astype(F32) + high_ref[at - half].astype(F32)).astype(
                BF16
            )


def merge(one, low, three, high):
    return kernel_call(
        merge_kernel,
        [in_vmem(value) for value in (one, low, three, high)],
        [IN_VMEM] * 4,
        [pltpu.VMEM(one.shape, BF16)] * 2,
        flops=one.size,
        moved=8 * one.size,
    )


def kv_kernel(shifts, tokens, same_ref, other_ref, merged_ref, biased_ref, *refs):
    outs = refs[tokens:]
    bias = biased_ref[:1]
    for at, by in enumerate(shifts):
        for second_by in range(SIDE):
            rank = rank_from_here(by, second_by)
            tile = wrap(rank // SIDE - lax.axis_index("group") // 2) * SIDE + lax.rem(rank, SIDE)
            tiles = [ref[hop, tile] for ref in (same_ref, other_ref) for hop in range(SIDE)]
            rows = jnp.concatenate(tiles, axis=0)
            part = jnp.dot(rows, merged_ref[...], preferred_element_type=F32)
            part = (part + bias).astype(BF16)
            if len(shifts) == 1:
                outs[second_by // 2][second_by % 2] = part
            else:
                outs[at][second_by] = part


def kv_partials(same, other, merged, biased):
    _, tiles, tile_rows, features = same.shape
    count = 2 * SIDE * tile_rows
    operands = [in_vmem(value) for value in (same, other, merged, biased)]

    def call(shifts, shapes, after):
        return kernel_call(
            functools.partial(kv_kernel, shifts, len(after)),
            [*operands, *after],
            [IN_VMEM] * 4 + [ANY] * len(after),
            [pltpu.VMEM((size, count, 2 * HEAD_DIM), BF16) for size in shapes],
            flops=len(shifts) * count * tiles * features * HEAD_DIM,
            moved=len(shifts) * 3 * 1024 * 1024,
        )

    low, high = call((2,), (2, 2), [])
    one, three, own = call((1, 3, 0), (SIDE,) * 3, [low])
    return low, high, one, three, own


def sum_kernel(*refs, sources, count):
    sources, outs = refs[:sources], refs[-count:]
    for at in range(count):
        total = sources[0][at].astype(F32)
        for source in sources[1:]:
            total = total + source[at].astype(F32)
        outs[at][...] = total.astype(BF16)


def sum_blocks(sources, after=()):
    count, rows, width = sources[0].shape
    return kernel_call(
        functools.partial(sum_kernel, sources=len(sources), count=count),
        [*map(in_vmem, sources), *after],
        [IN_VMEM] * len(sources) + [ANY] * len(after),
        [pltpu.VMEM((rows, width), BF16) for _ in range(count)],
        flops=len(sources) * sources[0].size,
        moved=10 * sources[0].size,
    )


def query_kernel(batch, *refs):
    parts, (weight_ref, out_ref) = refs[:SIDE], refs[SIDE:]
    total = jnp.zeros((batch, 1), F32)
    for part in parts:
        for at in range(SIDE):
            hidden = part[at, :batch, :].astype(F32)
            total += jnp.sum(hidden * hidden, axis=1, keepdims=True)
    inverse = lax.rsqrt(total / D + 1e-05)
    accum = jnp.zeros(out_ref.shape, F32)
    for part, far in zip(parts, HOPS):
        width = part.shape[2]
        for at, near in enumerate(HOPS):
            hidden = part[at, :batch, :].astype(F32)
            gain = part[at, batch : batch + 16, :].astype(F32)[:1]
            normed = (hidden * inverse * gain).astype(BF16)
            rank = rank_from_here(-near, -far)
            rows = pl.ds(pl.multiple_of(rank * width, width), width)
            accum += jnp.dot(normed, weight_ref[rows, :], preferred_element_type=F32)
    out_ref[...] = accum.astype(BF16)


def queries(parts, query_weight, batch):
    columns = query_weight.shape[1]
    return kernel_call(
        functools.partial(query_kernel, batch),
        [*map(in_vmem, parts), in_vmem(query_weight)],
        [IN_VMEM] * (SIDE + 1),
        pltpu.VMEM((batch, columns), BF16),
        flops=2 * batch * D * columns,
        moved=12 * 1024 * 1024,
    )


def attend_kernel(
    source_ref, count_ref, request_ref, query_ref, own_ref, other_ref, weight_ref, *outs
):
    batch, width = query_ref.shape
    half_rows = own_ref.shape[0]
    rows = 2 * half_rows
    slots = source_ref.shape[1]
    group = lax.axis_index("group")
    pair = lax.axis_index("pr")

    head = lax.axis_index("z") * 2 + lax.axis_index("xh")
    column = lax.broadcasted_iota(jnp.int32, (1, rows), 1) // (rows // slots)
    tile = jnp.zeros((1, rows), jnp.int32)
    for spot in range(slots):
        parity, far = spot // (slots // 2), spot % (slots // 2)
        encoder = wrap(head // 2 - HOPS[far % SIDE]) * 2 + lax.rem(head + far // SIDE, 2)
        tile = jnp.where(column == spot, encoder * 2 + lax.rem(parity + pair, 2), tile)
    owner = jnp.full((1, rows), -1, jnp.int32)
    for place in range(slots):
        request = place // MAXT
        valid = place % MAXT < count_ref[group * (slots // MAXT) + request]
        label = jnp.where(valid, request, -1)
        owner = jnp.where(tile == source_ref[group, place], label, owner)
    per_step = request_ref.shape[1]
    here = lax.broadcasted_iota(jnp.int32, (per_step, per_step), 0)
    there = lax.broadcasted_iota(jnp.int32, (per_step, per_step), 1)
    asked = jnp.where(here == there, request_ref[...], 0)
    asked = jnp.sum(asked, axis=1, keepdims=True)
    allowed = jnp.concatenate([asked] * (batch // per_step), axis=0) == owner

    keys = jnp.concatenate([own_ref[:, :HEAD_DIM], other_ref[:, :HEAD_DIM]], axis=0)
    values = jnp.concatenate([own_ref[:, HEAD_DIM:], other_ref[:, HEAD_DIM:]], axis=0)
    contexts = []
    for head in range(width // HEAD_DIM):
        span = slice(head * HEAD_DIM, (head + 1) * HEAD_DIM)
        scores = lax.dot_general(
            query_ref[:, span], keys, (((1,), (1,)), ((), ())), preferred_element_type=F32
        ) * (1.0 / HEAD_DIM**0.5)
        scores = jnp.where(allowed, scores, -1e30)
        largest = jnp.max(scores, axis=1, keepdims=True)
        weights = jnp.where(allowed, jnp.exp(scores - largest), 0.0)
        total = jnp.sum(weights, axis=1, keepdims=True)
        summed = jnp.dot(weights.astype(BF16), values, preferred_element_type=F32)
        contexts.append((summed / total).astype(BF16))
    context = jnp.concatenate(contexts, axis=1)
    columns = outs[0].shape[2]
    for first_by in range(SIDE):
        for second_by in range(SIDE):
            rank = rank_from_here(first_by, second_by)
            span = pl.ds(pl.multiple_of(rank * columns, columns), columns)
            branch = jnp.dot(context, weight_ref[:, span], preferred_element_type=F32)
            outs[first_by][second_by] = branch.astype(BF16)


def attend(tile_source, tile_count, row_request, query, own, other, out_weight):
    batch, width = query.shape
    columns = out_weight.shape[1] // (SIDE * SIDE)
    return kernel_call(
        attend_kernel,
        [tile_source, tile_count, row_request]
        + [in_vmem(value) for value in (query, own, other, out_weight)],
        [IN_SMEM, IN_SMEM] + [IN_VMEM] * 5,
        [pltpu.VMEM((SIDE, batch, columns), BF16) for _ in range(SIDE)],
        flops=2 * batch * width * out_weight.shape[1],
        moved=12 * 1024 * 1024,
        transcendentals=batch * 4 * 512,
    )


def mix_kernel(gate_ref, local_ref, *refs):
    sources, out_ref = refs[:SIDE], refs[SIDE]
    steps, batch, width = local_ref.shape
    gate = jnp.tanh(jnp.full((1, width), gate_ref[0, 0], F32))
    for step in range(steps):
        span = slice(step * batch, (step + 1) * batch)
        total = sources[0][span].astype(F32)
        for source in sources[1:]:
            total = total + source[span].astype(F32)
        out_ref[step] = (local_ref[step].astype(F32) + gate * total).astype(BF16)


def mix(gate, local, sources):
    return kernel_call(
        mix_kernel,
        [gate.reshape(1, 1), local, *map(in_vmem, sources)],
        [IN_SMEM, IN_VMEM] + [IN_VMEM] * SIDE,
        jax.ShapeDtypeStruct(local.shape, BF16),
        flops=SIDE * local.size,
        moved=12 * local.size,
    )


def body(
    vision_rows,
    tile_count,
    tile_source,
    row_request,
    proj_weight,
    proj_bias,
    kv_weight,
    query_weight,
    out_weight,
    norm_gain,
    attn_gate,
    states,
):
    groups = lax.axis_size("group")
    ranks = lax.axis_size(TP)
    tile_rows, features = vision_rows.shape[2:]
    per_group = vision_rows.shape[1] // groups
    slots = groups * per_group
    batch = STEPS * states.shape[1]
    width = states.shape[2]

    def spread(blocks, order):
        return [blocks[0]] + [shift(blocks[by], groups, order, by) for by in HOPS[1:]]

    def around(block, by):
        return lax.ppermute(block, "group", [(g, (g + 2 * by) % groups) for g in range(groups)])

    def first_sum(blocks, after=()):
        low, high, one, three, own = blocks
        low, high = shift(low, groups, FIRST, 1), shift(high, groups, FIRST, 3)
        up, down = merge(one, low, three, high)
        up, down = shift(up, groups, FIRST, 1), shift(down, groups, FIRST, 3)
        return sum_blocks([own, up, down], after)

    with jax.named_scope("contract"):
        *blocks, biased, carried, sent = contract(
            proj_weight, kv_weight, proj_bias, states, norm_gain, vision_rows
        )

    with jax.named_scope("load"):
        query_here, out_here = load(query_weight, out_weight, after=[carried])

    with jax.named_scope("gather_rows"):
        after, before = around(sent, 1), around(sent, 3)
        near = [sent, after, before, around(after, 1)]

    with jax.named_scope("contract"):
        merged = first_sum(blocks, [near[3], query_here, out_here])

    with jax.named_scope("gather_rows"):
        (same,) = join(
            near,
            [(i, 0, 0, i, 1) for i in range(SIDE)],
            [(SIDE, *vision_rows.shape[1:])],
            [merged[1]],
        )
        other = lax.ppermute(same, "group", [(g, g ^ 1) for g in range(groups)])

    with jax.named_scope("gather_states"):
        (carried,) = join(
            [carried[None]], [(0, 0, 0, 0, 1)], [(1, *carried.shape)], [other]
        )
        arrived = [shift(carried, groups, FIRST, by) for by in HOPS[1:]]

    with jax.named_scope("contract"):
        merged = [part[None] for part in spread(merged, SECOND)]
        (merged,) = sum_blocks(merged, after=[other, *arrived])

    with jax.named_scope("kv"):
        kv = kv_partials(same, other, merged, biased)

    with jax.named_scope("gather_states"):
        (states_near,) = join(
            [carried] + arrived,
            [(i, 0, 0, i, 1) for i in range(SIDE)],
            [(SIDE, *carried.shape[1:])],
        )
        parts = spread([states_near] * SIDE, SECOND)

    with jax.named_scope("kv"):
        kv = first_sum(kv, parts[1:3])
        query = queries(parts, query_here, batch)
        kv = [part[None] for part in spread(kv, SECOND)]
        (kv,) = sum_blocks(kv)
        halves = []
        for flip in range(2):
            pairs = []
            for g in range(groups):
                for t in range(ranks):
                    tile = (t // SIDE - g // 2) % SIDE * SIDE + t % SIDE
                    home = tile // 2 * ranks + 2 * g + (tile + flip) % 2
                    pairs.append((g * ranks + t, home))
            halves.append(lax.ppermute(kv, EVERY, pairs))

    with jax.named_scope("attend"):
        branch = attend(tile_source, tile_count, row_request, query, *halves, out_here)

    with jax.named_scope("mix"):
        branch = sum_blocks(spread(branch, FIRST))
        return mix(attn_gate, states, spread(branch, SECOND))


def solution(mesh):
    groups = mesh.shape["group"]
    split = Mesh(mesh.devices.reshape(groups, SIDE, 2, 2), ("group",) + TP)
    in_specs = (
        P("group", None, None, TP),
        P(),
        P(),
        P("group", None),
        P(None, TP),
        P(TP),
        P(None, TP, None),
        P(None, TP),
        P(TP, None),
        P(TP),
        P(),
        P(None, "group", TP),
    )
    out_specs = P(None, "group", TP)
    return jax.shard_map(body, mesh=split, in_specs=in_specs, out_specs=out_specs, check_vma=False)
```
